128 devices in a mesh: replica: 8 (over x, y_lo), shard: 16 (over z, y_hi, core).
Axes of the slice: x: 4, y: 4 (y_hi: 2, y_lo: 2; y = y_hi * 2 + y_lo), z: 4, core: 2. Of those that a mesh axis runs over, the one named last changes fastest.
Arguments:
- tokens: bfloat16 [65536, 4096], P(('replica', 'shard')), may hold values from -6 to 6
- cotangent: bfloat16 [65536, 2048], P(('replica', 'shard')), may hold values from -6 to 6
- next_weight: bfloat16 [8, 4096, 2048], P('replica', 'shard'), may hold values from -6 to 6
- inner_weight: float32 [8, 4096, 4096], P('replica', 'shard'), may hold values from -23 to 23
- outer_weight: float32 [4096, 4096], P('shard'), may hold values from -6 to 6
- momentum: float32 [4096, 4096], P('shard', 'replica'), may hold values from -1.8 to 1.8
Outputs:
- input_grad: bfloat16 [65536, 4096], P(('replica', 'shard'))
- weight_grad: float32 [8, 4096, 2048], P('replica', 'shard')
- new_outer: float32 [4096, 4096], P('shard', 'replica')
- new_momentum: float32 [4096, 4096], P('shard', 'replica')
- new_inner: bfloat16 [4096, 4096], P('shard')
The draws below stay inside these ranges and needn't reach their ends.
All inputs are finite; a program needn't handle non-finite values.
Results may differ from the reference program's by a relative error of at most 0.015.
Values may be sent and summed in bfloat16 or wider, within the bound.
No kernel may reach another device: no remote copies, remote signals or barrier semaphores. Data moves between devices by JAX's collectives and lax.ppermute only.
A program may use at most 192 MiB of HBM per device.

```python
import math
import jax
import jax.numpy as jnp
from jax import lax

D = 4096
SYNC_COLS = 4096
COLS = 2048
BLOCK = 128
TOK_DEV = 512
REPLICAS = 8
TOKENS = 65536
N_SHARD = 16


def shared_parts(key):
    outer = jax.random.truncated_normal(jax.random.fold_in(key, 101), -6.0, 6.0, (D, SYNC_COLS), jnp.float32)
    row_scale = jnp.exp(jax.random.uniform(jax.random.fold_in(key, 102), (D, 1), jnp.float32, math.log(0.3), math.log(3.0)))
    col_scale = jnp.exp(jax.random.uniform(jax.random.fold_in(key, 103), (1, SYNC_COLS), jnp.float32, math.log(0.3), math.log(3.0)))
    return (outer, row_scale, col_scale)


def draw_outer_weight(key, part):
    outer, row_scale, col_scale = shared_parts(key)
    return outer


def draw_inner_weight(key, part):
    outer, row_scale, col_scale = shared_parts(key)
    key = jax.random.fold_in(key, 2)
    noise = jax.random.truncated_normal(key, -6.0, 6.0, (REPLICAS, D, SYNC_COLS), jnp.float32)
    return outer[None] - 0.3 * noise * row_scale[None] * col_scale[None]


def shard_levels(own_key, extent, split, low, largest):
    def one(position, parts):
        heights = jax.random.uniform(jax.random.fold_in(jax.random.fold_in(own_key, 6), position), (parts,), jnp.float32, low / len(split), largest / len(split))
        return jnp.repeat(jnp.exp(heights), extent[position] // parts).reshape((-1,) + (1,) * (len(extent) - position - 1))

    loudness = one(*split[0])
    for cut in split[1:]:
        loudness = loudness * one(*cut)
    return loudness


def gaussian(own_key, shape, spread, most, cuts=(), dtype=jnp.bfloat16):
    drawn = spread * jax.random.normal(own_key, shape, jnp.float32)
    if cuts:
        drawn = drawn * shard_levels(own_key, shape, cuts, -0.22, 0.18)
    return jnp.clip(drawn, -most, most).astype(dtype)


def setup_inputs(seed: int = 0) -> dict:
    keys = jax.random.split(jax.random.key(seed), 7)
    return {
        "tokens": gaussian(keys[0], (TOKENS, D), 1.0, 6.0, ((0, 128),)),
        "cotangent": gaussian(keys[1], (TOKENS, COLS), 1.0, 6.0, ((0, 128),)),
        "next_weight": gaussian(keys[2], (REPLICAS, D, COLS), 1.0, 6.0, ((0, 8), (1, 16))),
        "inner_weight": draw_inner_weight(jax.random.fold_in(keys[6], 71), 0),
        "outer_weight": draw_outer_weight(jax.random.fold_in(keys[6], 71), 0),
        "momentum": gaussian(keys[5], (D, SYNC_COLS), 0.3, 1.8, ((0, 16), (1, 8)), jnp.float32),
    }


def reference(tokens, cotangent, next_weight, inner_weight, outer_weight, momentum):
    factor = D ** -0.5
    points = tokens.reshape(REPLICAS, N_SHARD, TOK_DEV, D)
    upstream = cotangent.reshape(REPLICAS, N_SHARD * TOK_DEV, COLS)

    def one_replica(inputs):
        feats, grads, weights = inputs
        flat = feats.reshape(N_SHARD * TOK_DEV, D)
        pre = jnp.dot(flat, weights, preferred_element_type=jnp.float32) * factor
        sig = jax.nn.sigmoid(pre)
        slope = (grads.astype(jnp.float32) * sig * (1.0 + pre * (1.0 - sig))).astype(jnp.bfloat16)
        back = (jnp.dot(slope, weights.T, preferred_element_type=jnp.float32) * factor).astype(jnp.bfloat16)
        groups = slope.reshape(N_SHARD, TOK_DEV, COLS)

        def add_term(total, pair):
            group_feats, group_slope = pair
            term = jnp.dot(group_feats.T, group_slope, preferred_element_type=jnp.float32)
            term = lax.optimization_barrier(term.astype(jnp.bfloat16)).astype(jnp.float32)
            return total + term, None

        summed, unused = lax.scan(add_term, jnp.zeros((D, COLS), jnp.float32), (feats, groups))
        return back, summed * factor

    back, weight_grad = lax.map(one_replica, (points, upstream, next_weight))
    input_grad = back.reshape(TOKENS, D)

    delta = (outer_weight[None] - inner_weight).reshape(REPLICAS, D, SYNC_COLS // BLOCK, BLOCK)
    top = jnp.max(jnp.abs(delta), axis=3) + 1e-6
    scale_back = lax.optimization_barrier(top.astype(jnp.bfloat16)).astype(jnp.float32)
    codes = (delta / scale_back[..., None]).astype(jnp.bfloat16)
    decoded = codes.astype(jnp.float32) * scale_back[..., None]
    average = jnp.sum(decoded, axis=0).reshape(D, SYNC_COLS) / REPLICAS
    new_momentum = 0.9 * momentum + average
    new_outer = outer_weight - 0.7 * (average + 0.9 * new_momentum)
    new_inner = new_outer.astype(jnp.bfloat16)
    return input_grad, weight_grad, new_outer, new_momentum, new_inner
```

```python
import functools

import jax
import jax.numpy as jnp
from jax import lax
from jax.experimental import pallas as pl
from jax.experimental.pallas import tpu as pltpu
from jax.sharding import PartitionSpec as P

F32 = jnp.float32
BF16 = jnp.bfloat16
MIB = 1 << 20

NZ, NY, NC, NX, NL = 4, 2, 2, 4, 2
DIRS = [(dz, dy) for dz in range(NZ) for dy in range(NY)]


def shard_perm(dz, dy, dc):
    perm = []
    for i in range(NZ * NY * NC):
        z, y, c = i // (NY * NC), (i // NC) % NY, i % NC
        j = ((z + dz) % NZ) * NY * NC + ((y + dy) % NY) * NC + (c + dc) % NC
        perm.append((i, j))
    return perm


def replica_perm(dx, dl):
    perm = []
    for i in range(NX * NL):
        x, w = i // NL, i % NL
        perm.append((i, ((x + dx) % NX) * NL + (w + dl) % NL))
    return perm


def to_zp(a):
    return lax.ppermute(a, "shard", shard_perm(1, 0, 0))


def to_zm(a):
    return lax.ppermute(a, "shard", shard_perm(-1, 0, 0))


def to_y(a):
    return lax.ppermute(a, "shard", shard_perm(0, 1, 0))


def to_core(a):
    return lax.ppermute(a, "shard", shard_perm(0, 0, 1))


def to_x(a, dx):
    return lax.ppermute(a, "replica", replica_perm(dx, 0))


def to_l(a):
    return lax.ppermute(a, "replica", replica_perm(0, 1))


def add(*terms):
    total = terms[0].astype(F32)
    for term in terms[1:]:
        total = total + term.astype(F32)
    return total


def whole(shape):
    return pl.BlockSpec(shape, lambda i, *_: (0,) * len(shape))


def cost(flops, nbytes, trans=0):
    return pl.CostEstimate(flops=int(flops), bytes_accessed=int(nbytes), transcendentals=int(trans))


def params(mib):
    return pltpu.CompilerParams(vmem_limit_bytes=mib * MIB)


def decode_kernel(pos_ref, outer_ref, inner_ref, *out_refs):
    dx = pl.program_id(0)
    width = outer_ref.shape[1]
    for g in range(width // 128):
        cols = slice(g * 128, (g + 1) * 128)
        delta = outer_ref[:, cols] - inner_ref[0, :, cols]
        top = jnp.max(jnp.abs(delta), axis=1, keepdims=True) + 1e-06
        scale = top.astype(BF16).astype(F32)
        code = (delta / scale).astype(BF16).astype(F32)
        decoded = (code * scale).astype(BF16)
        for k, out_ref in enumerate(out_refs):
            @pl.when(dx == k)
            def _(out_ref=out_ref, decoded=decoded, cols=cols):
                out_ref[:, cols] = decoded


def decode(x_pos, outer, inner):
    rows, cols = outer.shape
    width = cols // NX
    return pl.pallas_call(
        decode_kernel,
        grid_spec=pltpu.PrefetchScalarGridSpec(
            num_scalar_prefetch=1,
            grid=(NX,),
            in_specs=[
                pl.BlockSpec((rows, width), lambda i, p: (0, lax.rem(p[0] + i, NX))),
                pl.BlockSpec((1, rows, width), lambda i, p: (0, 0, lax.rem(p[0] + i, NX))),
            ],
            out_specs=[whole((rows, width))] * NX,
        ),
        out_shape=[jax.ShapeDtypeStruct((rows, width), BF16)] * NX,
        compiler_params=params(32),
        cost_estimate=cost(10 * rows * cols, 10 * rows * cols),
        name="decode",
    )(x_pos, outer, inner)


def slope_kernel(factor, npieces, off_ref, xo_ref, xp_ref, co_ref, cp_ref, *refs):
    piece_refs, so_ref, sp_ref = refs[:npieces], refs[npieces], refs[npieces + 1]
    for x_ref, cot_ref, out_ref in ((xo_ref, co_ref, so_ref), (xp_ref, cp_ref, sp_ref)):
        pre = None
        for k in range(npieces):
            depth = piece_refs[k].shape[0]
            cols = pl.ds(pl.multiple_of(off_ref[k], 256), depth)
            term = jnp.dot(x_ref[:, cols], piece_refs[k][...], preferred_element_type=F32)
            pre = term if pre is None else pre + term
        pre = pre * factor
        sig = 1.0 / (1.0 + jnp.exp(-pre))
        out_ref[...] = (cot_ref[...].astype(F32) * sig * (1.0 + pre * (1.0 - sig))).astype(BF16)


def slope_of(factor, offs, cot_block, x_own, x_par, cot_own, cot_par, j, pieces):
    toks, feats = x_own.shape
    width = pieces[0].shape[1]
    tile = 256
    n = len(pieces)
    scalars = jnp.concatenate([offs, cot_block[None]]).astype(jnp.int32)
    return pl.pallas_call(
        functools.partial(slope_kernel, factor, n),
        grid_spec=pltpu.PrefetchScalarGridSpec(
            num_scalar_prefetch=1,
            grid=(toks // tile,),
            in_specs=[
                pl.BlockSpec((tile, feats), lambda i, s: (i, 0)),
                pl.BlockSpec((tile, feats), lambda i, s: (i, 0)),
                pl.BlockSpec((tile, width), lambda i, s: (i, s[n])),
                pl.BlockSpec((tile, width), lambda i, s: (i, j)),
            ] + [whole(p.shape) for p in pieces],
            out_specs=[pl.BlockSpec((tile, width), lambda i, s: (i, 0))] * 2,
        ),
        out_shape=[jax.ShapeDtypeStruct((toks, width), BF16)] * 2,
        compiler_params=params(48),
        cost_estimate=cost(4 * toks * feats * width, 4 * toks * feats + 2 * feats * width, 2 * toks * width),
        name="slope",
    )(scalars, x_own, x_par, cot_own, cot_par, *pieces)


def wgrad_kernel(blk_ref, xo_ref, xp_ref, so_ref, sp_ref, *out_refs):
    d = pl.program_id(0)
    dims = (((0,), (0,)), ((), ()))
    term = lax.dot_general(xo_ref[...], so_ref[...], dims, preferred_element_type=F32)
    term = term + lax.dot_general(xp_ref[...], sp_ref[...], dims, preferred_element_type=F32)
    term = term.astype(BF16)
    for k, out_ref in enumerate(out_refs):
        @pl.when(d == k)
        def _(out_ref=out_ref):
            out_ref[...] = term


def wgrad_of(blks, x_own, x_par, s_own, s_par):
    toks, feats = x_own.shape
    width = s_own.shape[1]
    n = blks.shape[0]
    rows = feats // (NZ * NY)
    return pl.pallas_call(
        wgrad_kernel,
        grid_spec=pltpu.PrefetchScalarGridSpec(
            num_scalar_prefetch=1,
            grid=(n,),
            in_specs=[
                pl.BlockSpec((toks, rows), lambda i, b: (0, b[i])),
                pl.BlockSpec((toks, rows), lambda i, b: (0, b[i])),
                whole((toks, width)),
                whole((toks, width)),
            ],
            out_specs=[whole((rows, width))] * n,
        ),
        out_shape=[jax.ShapeDtypeStruct((rows, width), BF16)] * n,
        compiler_params=params(32),
        cost_estimate=cost(4 * toks * n * rows * width, 4 * toks * n * rows + 2 * n * rows * width),
        name="wgrad",
    )(blks, x_own, x_par, s_own, s_par)


def igrad_kernel(factor, na, nb, has_term, off_ref, sa_ref, sb_ref, *refs):
    a_refs, b_refs = refs[:na], refs[na:na + nb]
    term_ref = refs[na + nb] if has_term else None
    out_ref = refs[-1]
    dims = (((1,), (1,)), ((), ()))
    sa, sb = sa_ref[...], sb_ref[...]
    k = 0
    for a_ref in a_refs:
        depth = a_ref.shape[0]
        cols = pl.ds(pl.multiple_of(off_ref[k], 256), depth)
        total = lax.dot_general(sa, a_ref[...], dims, preferred_element_type=F32)
        if has_term:
            total = total + term_ref[:, cols].astype(F32)
        first, filled = k, 0
        parts = []
        while filled < depth:
            b_ref = b_refs[k]
            parts.append(lax.dot_general(sb, b_ref[...], dims, preferred_element_type=F32))
            filled += b_ref.shape[0]
            k += 1
        total = total + (parts[0] if len(parts) == 1 else jnp.concatenate(parts, axis=1))
        if has_term:
            total = total * factor
        out_ref[:, cols] = total.astype(BF16)


def igrad_of(factor, offs, s_a, s_b, a, b, term):
    toks, width = s_a.shape
    feats = sum(p.shape[0] for p in a)
    tile = 256
    extra = [] if term is None else [term]
    return pl.pallas_call(
        functools.partial(igrad_kernel, factor, len(a), len(b), term is not None),
        grid_spec=pltpu.PrefetchScalarGridSpec(
            num_scalar_prefetch=1,
            grid=(toks // tile,),
            in_specs=[pl.BlockSpec((tile, width), lambda i, s: (i, 0))] * 2
            + [whole(p.shape) for p in list(a) + list(b)]
            + [pl.BlockSpec((tile, feats), lambda i, s: (i, 0)) for _ in extra],
            out_specs=pl.BlockSpec((tile, feats), lambda i, s: (i, 0)),
        ),
        out_shape=jax.ShapeDtypeStruct((toks, feats), BF16),
        compiler_params=params(48),
        cost_estimate=cost(4 * toks * feats * width, 2 * toks * feats + 4 * feats * width),
        name="igrad",
    )(offs, s_a, s_b, *a, *b, *extra)


def by_core(core, mine, other, axis):
    return jnp.where(
        core == 0,
        jnp.concatenate([mine, other], axis=axis),
        jnp.concatenate([other, mine], axis=axis),
    )


def shards(tokens, cotangent, next_weight, inner_weight, outer_weight, momentum):
    toks, feats = tokens.shape
    factor = feats ** (-0.5)
    me = lax.axis_index("shard")
    z, y, core = me // (NY * NC), (me // NC) % NY, me % NC
    pos = lax.axis_index("replica")
    x, low = pos // NL, pos % NL

    blk = {(dz, dy): ((z + dz) % NZ) * NY + (y + dy) % NY for dz, dy in DIRS}
    rows = feats // (NZ * NY)
    half = rows // 2
    cols = next_weight.shape[2] // NC
    chunk = cols // 2
    my_rows = next_weight[0]

    keep = lax.dynamic_slice_in_dim(my_rows, core * cols, cols, 1)
    give = lax.dynamic_slice_in_dim(my_rows, (1 - core) * cols, cols, 1)
    got = to_core(give)
    a0 = by_core(core, keep[:, :chunk], got[:, :chunk], 0)
    b0 = by_core(core, keep[:, chunk:], got[:, chunk:], 0)

    a, b = {(0, 0): a0}, {(0, 0): [b0]}
    a[0, 1] = to_y(a0)
    b[3, 0] = [to_zp(b0)]
    b[1, 0] = [to_zm(b0)]
    a[3, 0] = to_zp(a0)
    a[1, 0] = to_zm(a0)
    b[2, 0] = [to_zp(b[3, 0][0][:half]), to_zm(b[1, 0][0][half:])]
    a[3, 1] = to_zp(a[0, 1])
    a[1, 1] = to_zm(a[0, 1])
    a[2, 0] = to_zp(a[3, 0])
    a[2, 1] = to_zm(a[1, 1])
    for dz in (0, 3, 1, 2):
        b[dz, 1] = [to_y(part) for part in b[dz, 0]]

    x_par = to_core(tokens)
    cot_par = to_core(lax.dynamic_slice_in_dim(cotangent, (1 - core) * cols, cols, 1))

    a_list = [a[d] for d in DIRS]
    b_list = [part for d in DIRS for part in b[d]]
    a_offs = jnp.stack([blk[d] * rows for d in DIRS]).astype(jnp.int32)
    b_offs = jnp.stack(
        [blk[d] * rows + (h * half) for d in DIRS for h in range(len(b[d]))]
    ).astype(jnp.int32)
    blks = jnp.stack([blk[d] for d in DIRS]).astype(jnp.int32)

    dec = decode(x[None].astype(jnp.int32), outer_weight, inner_weight)
    rec = [to_x(dec[dx], dx) for dx in (1, 2, 3)]
    x_sum = add(dec[0], *rec)
    share = momentum.shape[1]
    mine = lax.dynamic_slice_in_dim(x_sum, low * share, share, 1)
    other = lax.dynamic_slice_in_dim(x_sum, (1 - low) * share, share, 1)
    total = mine + to_l(other.astype(BF16)).astype(F32)
    average = total / (NX * NL)
    outer_share = lax.dynamic_slice_in_dim(outer_weight, pos * share, share, 1)
    new_momentum = 0.9 * momentum + average
    new_outer = outer_share - 0.7 * (average + 0.9 * new_momentum)
    inner_share = new_outer.astype(BF16)
    inner_pair = by_core(low, inner_share, to_l(inner_share), 1)
    new_inner = jnp.zeros(outer_weight.shape, BF16)
    for dx in range(NX):
        part = inner_pair if dx == 0 else to_x(inner_pair, dx)
        at = ((x - dx) % NX) * (share * NL)
        new_inner = lax.dynamic_update_slice_in_dim(new_inner, part, at, 1)

    sa_own, sa_par = slope_of(
        factor, a_offs, core * 2, tokens, x_par, cotangent, cot_par, 0, a_list
    )
    ga = dict(zip(DIRS, wgrad_of(blks, tokens, x_par, sa_own, sa_par)))
    sb_own, sb_par = slope_of(
        factor, b_offs, core * 2 + 1, tokens, x_par, cotangent, cot_par, 1, b_list
    )
    gb = dict(zip(DIRS, wgrad_of(blks, tokens, x_par, sb_own, sb_par)))

    t0 = to_zm(ga[2, 0])
    t1 = to_zp(ga[2, 1])
    up0 = to_zp(ga[1, 0])
    down1 = to_zm(ga[3, 1])
    down0 = to_zm(add(ga[3, 0], t0).astype(BF16))
    up1 = to_zp(add(ga[1, 1], t1).astype(BF16))
    sum1 = add(ga[0, 1], down1, up1).astype(BF16)
    a_sum = add(ga[0, 0], down0, up0, to_y(sum1))

    hb = {dz: add(gb[dz, 0], to_y(gb[dz, 1])) for dz in (2, 3, 1, 0)}
    top = to_zm(hb[2][:half].astype(BF16))
    bot = to_zp(hb[2][half:].astype(BF16))
    down = to_zm(
        jnp.concatenate([add(hb[3][:half], top), hb[3][half:]], axis=0).astype(BF16)
    )
    up = to_zp(
        jnp.concatenate([hb[1][:half], add(hb[1][half:], bot)], axis=0).astype(BF16)
    )
    b_sum = add(hb[0], down, up)

    def split(total_sum):
        keep_rows = lax.dynamic_slice_in_dim(total_sum, core * half, half, 0)
        give_rows = lax.dynamic_slice_in_dim(total_sum, (1 - core) * half, half, 0)
        return keep_rows * factor, to_core(give_rows) * factor

    a_mine, a_got = split(a_sum)
    b_mine, b_got = split(b_sum)
    weight_grad = by_core(
        core,
        jnp.concatenate([a_mine, b_mine], axis=1),
        jnp.concatenate([a_got, b_got], axis=1),
        1,
    )[None]

    part = igrad_of(factor, b_offs, sa_par, sb_par, a_list, b_list, None)
    input_grad = igrad_of(factor, b_offs, sa_own, sb_own, a_list, b_list, to_core(part))
    return (input_grad, weight_grad, new_outer, new_momentum, new_inner)


def solution(mesh):
    return jax.shard_map(
        shards,
        mesh=mesh,
        in_specs=(
            P(("replica", "shard"), None),
            P(("replica", "shard"), None),
            P("replica", "shard", None),
            P("replica", "shard", None),
            P("shard", None),
            P("shard", "replica"),
        ),
        out_specs=(
            P(("replica", "shard"), None),
            P("replica", "shard", None),
            P("shard", "replica"),
            P("shard", "replica"),
            P("shard", None),
        ),
        check_vma=False,
    )
```

```python
import functools

import jax
import jax.numpy as jnp
from jax import lax
from jax.experimental import pallas as pl
from jax.experimental.pallas import tpu as pltpu
from jax.sharding import PartitionSpec as P

F32 = jnp.float32
BF16 = jnp.bfloat16
MIB = 1 << 20
COST = 0.3

NZ, NY, NC, NX, NL = 4, 2, 2, 4, 2
DIRS = [(dz, dy) for dz in range(NZ) for dy in range(NY)]


def shard_perm(dz, dy, dc):
    perm = []
    for i in range(NZ * NY * NC):
        z, y, c = i // (NY * NC), (i // NC) % NY, i % NC
        j = ((z + dz) % NZ) * NY * NC + ((y + dy) % NY) * NC + (c + dc) % NC
        perm.append((i, j))
    return perm


def to_zp(a):
    return lax.ppermute(a, "shard", shard_perm(1, 0, 0))


def to_zm(a):
    return lax.ppermute(a, "shard", shard_perm(-1, 0, 0))


def to_y(a):
    return lax.ppermute(a, "shard", shard_perm(0, 1, 0))


def to_core(a):
    return lax.ppermute(a, "shard", shard_perm(0, 0, 1))


def to_l(a):
    return lax.ppermute(a, "replica", [(i, i ^ 1) for i in range(NX * NL)])


def to_near(a):
    return lax.ppermute(a, "replica", [(i, i ^ NL) for i in range(NX * NL)])


def to_far(a):
    perm = [(i, (NX - 1 - i // NL) * NL + i % NL) for i in range(NX * NL)]
    return lax.ppermute(a, "replica", perm)


def add(*terms):
    total = terms[0].astype(F32)
    for term in terms[1:]:
        total = total + term.astype(F32)
    return total


def whole(shape):
    return pl.BlockSpec(shape, lambda i, *_: (0,) * len(shape))


def cost(flops, nbytes, trans=0):
    return pl.CostEstimate(
        flops=int(COST * flops), bytes_accessed=int(COST * nbytes), transcendentals=int(COST * trans)
    )


def params(mib):
    return pltpu.CompilerParams(vmem_limit_bytes=mib * MIB)


def decode_kernel(order_ref, outer_ref, inner_ref, own_ref, far_ref, near_ref):
    step = pl.program_id(0)
    width = outer_ref.shape[1]
    decoded = []
    for g in range(width // 128):
        cols = slice(g * 128, (g + 1) * 128)
        delta = outer_ref[:, cols] - inner_ref[0, :, cols]
        top = jnp.max(jnp.abs(delta), axis=1, keepdims=True) + 1e-06
        scale = top.astype(BF16).astype(F32)
        code = (delta / scale).astype(BF16).astype(F32)
        decoded.append((code * scale).astype(BF16))
    decoded = jnp.concatenate(decoded, axis=1)

    @pl.when(step == 0)
    def _():
        own_ref[...] = decoded

    @pl.when(step == 1)
    def _():
        far_ref[...] = decoded

    @pl.when(step >= 2)
    def _():
        near_ref[0] = decoded


def decode(order, outer, inner):
    rows, cols = outer.shape
    width = cols // NX
    one = jax.ShapeDtypeStruct((rows, width), BF16)
    return pl.pallas_call(
        decode_kernel,
        grid_spec=pltpu.PrefetchScalarGridSpec(
            num_scalar_prefetch=1,
            grid=(NX,),
            in_specs=[
                pl.BlockSpec((rows, width), lambda i, p: (0, p[i])),
                pl.BlockSpec((1, rows, width), lambda i, p: (0, 0, p[i])),
            ],
            out_specs=[whole((rows, width))] * 2
            + [pl.BlockSpec((1, rows, width), lambda i, p: (jnp.maximum(i - 2, 0), 0, 0))],
        ),
        out_shape=[one, one, jax.ShapeDtypeStruct((2, rows, width), BF16)],
        compiler_params=params(32),
        cost_estimate=cost(10 * rows * cols, 10 * rows * cols),
        name="decode",
    )(order, outer, inner)


def pre_kernel(factor, counts, has_sum, last, off_ref, *refs):
    n = len(counts)
    refs = list(refs)
    x_refs = [refs.pop(0) for _ in range(2)]
    pieces = [refs.pop(0) for _ in range(n)]
    sums = [refs.pop(0) for _ in range(2)] if has_sum else [None, None]
    cots = [refs.pop(0) for _ in range(2)] if last else [None, None]
    for x_ref, sum_ref, cot_ref, out_ref in zip(x_refs, sums, cots, refs):
        pre = sum_ref[...] if has_sum else None
        at = 0
        for piece, count in zip(pieces, counts):
            depth = piece.shape[0] // count
            for part in range(count):
                cols = pl.ds(pl.multiple_of(off_ref[at], 256), depth)
                rows = piece[part * depth:(part + 1) * depth]
                term = jnp.dot(x_ref[:, cols], rows, preferred_element_type=F32)
                pre = term if pre is None else pre + term
                at += 1
        if last:
            pre = pre * factor
            sig = 0.5 + 0.5 * jnp.tanh(0.5 * pre)
            pre = (cot_ref[...].astype(F32) * sig * (1.0 + pre * (1.0 - sig))).astype(BF16)
        out_ref[...] = pre


def pre_of(factor, x_pair, pieces, counts, offs, sums=None, cots=None, cot_block=None):
    toks, feats = x_pair[0].shape
    width = pieces[0].shape[1]
    depth = sum(p.shape[0] for p in pieces)
    tile = toks // 2
    n = len(offs)
    scalars = jnp.stack(list(offs) + [0 if cot_block is None else cot_block]).astype(jnp.int32)
    row = pl.BlockSpec((tile, width), lambda i, s: (i, 0))
    in_specs = [pl.BlockSpec((tile, feats), lambda i, s: (i, 0))] * 2
    in_specs += [whole(p.shape) for p in pieces]
    args = list(x_pair) + list(pieces)
    if sums is not None:
        in_specs += [row, row]
        args += list(sums)
    if cots is not None:
        in_specs += [pl.BlockSpec((tile, width), lambda i, s: (i, s[n])), row]
        args += list(cots)
    last = cots is not None
    return pl.pallas_call(
        functools.partial(pre_kernel, factor, counts, sums is not None, last),
        grid_spec=pltpu.PrefetchScalarGridSpec(
            num_scalar_prefetch=1,
            grid=(toks // tile,),
            in_specs=in_specs,
            out_specs=[row, row],
        ),
        out_shape=[jax.ShapeDtypeStruct((toks, width), BF16 if last else F32)] * 2,
        compiler_params=params(60 if last else 48),
        cost_estimate=cost(4 * toks * depth * width, 4 * toks * feats + 2 * depth * width + 8 * toks * width),
        name="slope" if last else "pre",
    )(scalars, *args)


def wgrad_kernel(halves, blk_ref, xo_ref, xp_ref, so_ref, sp_ref, *out_refs):
    step = pl.program_id(0)
    dims = (((0,), (0,)), ((), ()))
    term = lax.dot_general(xo_ref[...], so_ref[...], dims, preferred_element_type=F32)
    term = term + lax.dot_general(xp_ref[...], sp_ref[...], dims, preferred_element_type=F32)
    term = term.astype(BF16)
    out_refs = list(out_refs)
    for k, halved in enumerate(halves):
        mine = [out_refs.pop(0) for _ in range(2 if halved else 1)]

        @pl.when(step == k)
        def _(mine=mine):
            at = 0
            for ref in mine:
                ref[...] = term[at:at + ref.shape[0]]
                at += ref.shape[0]


def wgrad_of(blks, halves, x_pair, slopes):
    toks, feats = x_pair[0].shape
    width = slopes[0].shape[1]
    n = len(blks)
    rows = feats // (NZ * NY)
    shapes = []
    for halved in halves:
        shapes += [(rows // 2, width)] * 2 if halved else [(rows, width)]
    outs = pl.pallas_call(
        functools.partial(wgrad_kernel, halves),
        grid_spec=pltpu.PrefetchScalarGridSpec(
            num_scalar_prefetch=1,
            grid=(n,),
            in_specs=[pl.BlockSpec((toks, rows), lambda i, b: (0, b[i]))] * 2
            + [whole((toks, width))] * 2,
            out_specs=[whole(s) for s in shapes],
        ),
        out_shape=[jax.ShapeDtypeStruct(s, BF16) for s in shapes],
        compiler_params=params(48),
        cost_estimate=cost(4 * toks * n * rows * width, 4 * toks * n * rows + 2 * n * rows * width),
        name="wgrad",
    )(jnp.stack(blks).astype(jnp.int32), *x_pair, *slopes)
    outs = list(outs)
    return [[outs.pop(0) for _ in range(2)] if halved else outs.pop(0) for halved in halves]


def igrad_kernel(factor, counts, has_term, off_ref, s_ref, *refs):
    out_ref = refs[-1]
    n = len(counts)
    at = 0
    dims = (((1,), (1,)), ((), ()))
    for piece, count in zip(refs[:n], counts):
        depth = piece.shape[0] // count
        for part in range(count):
            cols = pl.ds(pl.multiple_of(off_ref[at], 256), depth)
            rows = piece[part * depth:(part + 1) * depth]
            total = lax.dot_general(s_ref[...], rows, dims, preferred_element_type=F32)
            if has_term:
                total = (total + refs[n][:, cols].astype(F32)) * factor
            out_ref[:, cols] = total.astype(BF16)
            at += 1


def igrad_of(factor, counts, offs, slope, pieces, term=None):
    toks, width = slope.shape
    feats = sum(p.shape[0] for p in pieces)
    tile = toks // 2
    extra = [] if term is None else [term]
    return pl.pallas_call(
        functools.partial(igrad_kernel, factor, counts, term is not None),
        grid_spec=pltpu.PrefetchScalarGridSpec(
            num_scalar_prefetch=1,
            grid=(toks // tile,),
            in_specs=[pl.BlockSpec((tile, width), lambda i, s: (i, 0))]
            + [whole(p.shape) for p in pieces]
            + [pl.BlockSpec((tile, feats), lambda i, s: (i, 0)) for _ in extra],
            out_specs=pl.BlockSpec((tile, feats), lambda i, s: (i, 0)),
        ),
        out_shape=jax.ShapeDtypeStruct((toks, feats), BF16),
        compiler_params=params(48),
        cost_estimate=cost(2 * toks * feats * width, 2 * toks * feats + 2 * feats * width),
        name="igrad",
    )(jnp.stack(offs).astype(jnp.int32), slope, *pieces, *extra)


def by_core(core, mine, other, axis):
    return jnp.where(
        core == 0,
        jnp.concatenate([mine, other], axis=axis),
        jnp.concatenate([other, mine], axis=axis),
    )


def place_kernel(order_ref, own_ref, near_ref, out_ref):
    step = pl.program_id(0)

    @pl.when(step < 2)
    def _():
        out_ref[...] = own_ref[0]

    @pl.when(step >= 2)
    def _():
        out_ref[...] = near_ref[0]


def side_by_side(order, own, near):
    half, rows, width = own.shape
    n = 2 * half
    return pl.pallas_call(
        place_kernel,
        grid_spec=pltpu.PrefetchScalarGridSpec(
            num_scalar_prefetch=1,
            grid=(n,),
            in_specs=[
                pl.BlockSpec((1, rows, width), lambda i, p: (jnp.minimum(i, 1), 0, 0)),
                pl.BlockSpec((1, rows, width), lambda i, p: (jnp.maximum(i - 2, 0), 0, 0)),
            ],
            out_specs=pl.BlockSpec((rows, width), lambda i, p: (0, p[i])),
        ),
        out_shape=jax.ShapeDtypeStruct((rows, n * width), own.dtype),
        compiler_params=params(32),
        cost_estimate=cost(0, 4 * n * rows * width),
        name="place",
    )(order, own, near)


def hold(a, *deps):
    return lax.optimization_barrier((a,) + deps)[0]


def shards(tokens, cotangent, next_weight, inner_weight, outer_weight, momentum):
    toks, feats = tokens.shape
    factor = feats ** (-0.5)
    me = lax.axis_index("shard")
    z, y, core = me // (NY * NC), (me // NC) % NY, me % NC
    pos = lax.axis_index("replica")
    low = pos % NL
    x = pos // NL
    near = x + 1 - 2 * (x % 2)
    order = jnp.stack([x, NX - 1 - x, near, NX - 1 - near]).astype(jnp.int32)

    blk = {(dz, dy): ((z + dz) % NZ) * NY + (y + dy) % NY for dz, dy in DIRS}
    rows = feats // (NZ * NY)
    half = rows // 2
    cols = next_weight.shape[2] // NC

    def offs(*dirs):
        out = []
        for d in dirs:
            at = blk[d[:2]] * rows
            out.append(at + half if d[2:] == (1,) else at)
        return out

    keep = lax.dynamic_slice_in_dim(next_weight[0], core * cols, cols, 1)
    give = lax.dynamic_slice_in_dim(next_weight[0], (1 - core) * cols, cols, 1)
    w00 = by_core(core, keep, to_core(give), 0)

    w30, w10 = to_zp(w00), to_zm(w00)
    a01, b01 = to_y(w00[:half]), to_y(w00[half:])
    x_pair = (tokens, to_core(hold(tokens, w00)))
    own_dec, far_dec, near_dec = decode(order, hold(outer_weight, w00), inner_weight)
    near_got = to_near(hold(near_dec, x_pair[1], a01))
    a01h = hold(a01, own_dec)
    a31, a11 = to_zp(a01h), to_zm(a01h)
    b20 = to_zm(w10[half:])
    b31_b11 = to_y(hold(jnp.concatenate([w30[half:], w10[half:]], axis=0), b01))
    a20 = to_zp(w30[:half])

    first, first_counts = [w00, w30, w10, a01, b01], [1] * 5
    first_offs = offs((0, 0), (3, 0), (1, 0), (0, 1), (0, 1, 1))
    sums = pre_of(factor, x_pair, first, first_counts, first_offs)
    a21 = to_zm(hold(a11, sums[0]))
    b21 = to_y(hold(b20, sums[0], b31_b11))
    far_send = add(far_dec, hold(near_got, sums[0])[1]).astype(BF16)
    far_got = to_far(far_send)
    cot_give = lax.dynamic_slice_in_dim(cotangent, (1 - core) * cols, cols, 1)
    cots = (cotangent, to_core(hold(cot_give, sums[0])))
    second, second_counts = [a20, b20, a31, b31_b11, a11], [1, 1, 1, 2, 1]
    second_offs = offs((2, 0), (2, 0, 1), (3, 1), (3, 1, 1), (1, 1, 1), (1, 1))
    sums = pre_of(
        factor, x_pair, second, second_counts, second_offs, (hold(sums[0], far_send), sums[1])
    )

    share = momentum.shape[1]

    def share_of(a, which):
        return lax.dynamic_slice_in_dim(a, which * share, share, 1)

    x_terms = (own_dec, near_got[0], hold(far_got, sums[0]))
    other = add(*[share_of(a, 1 - low) for a in x_terms]).astype(BF16)
    third, third_offs = [a21, b21], offs((2, 1), (2, 1, 1))
    slopes = pre_of(
        factor, x_pair, third, [1, 1], third_offs, (hold(sums[0], other), sums[1]), cots, core
    )
    got = hold(to_l(other), slopes[0])
    average = add(*[share_of(a, low) for a in x_terms], got) / (NX * NL)
    outer_share = lax.dynamic_slice_in_dim(outer_weight, pos * share, share, 1)
    new_momentum = 0.9 * momentum + average
    new_outer = outer_share - 0.7 * (average + 0.9 * new_momentum)
    inner_share = new_outer.astype(BF16)
    inner_other = to_l(inner_share)

    early, late = [(2, 1), (3, 1)], [(1, 1), (2, 0), (3, 0), (1, 0), (0, 1), (0, 0)]
    g21, g31 = wgrad_of(
        [blk[d] for d in early], (False,) * 2, x_pair, (hold(slopes[0], inner_share), slopes[1])
    )
    inner_pair = by_core(low, inner_share, hold(inner_other, g21), 1)
    inner_far = to_far(inner_pair)

    r31, r21 = to_zm(g31), to_zp(g21)
    late_slopes = (hold(slopes[0], inner_pair), slopes[1])
    g11, g20, g30, g10, g01, g00 = wgrad_of(
        [blk[d] for d in late], (False,) * 6, x_pair, late_slopes
    )

    s11 = add(g11, r21).astype(BF16)
    r11, r20 = to_zp(s11), to_zm(hold(g20, r31))
    inner_own = jnp.stack([inner_pair, inner_far])
    inner_near = to_near(inner_own)
    pieces, counts = first + second + third, first_counts + second_counts + [1, 1]
    piece_offs = first_offs + second_offs + third_offs
    part = igrad_of(factor, counts, piece_offs, hold(slopes[1], s11, r31, inner_own), pieces)

    s30 = add(g30, hold(r20, part)).astype(BF16)
    s01 = add(g01, r31, hold(r11, part, inner_near)).astype(BF16)
    t30, t01, t10 = to_zm(s30), to_y(s01), to_zp(hold(g10, s01))
    part_got = to_core(hold(part, s30, s01))
    input_grad = igrad_of(
        factor, counts, piece_offs, hold(slopes[0], s30, s01, inner_near), pieces, part_got
    )
    new_inner = side_by_side(order, hold(inner_own, input_grad), inner_near)
    g00 = hold(g00, input_grad, new_inner)

    def rows_of(which):
        terms = [lax.dynamic_slice_in_dim(a, which * half, half, 0) for a in (g00, t30, t10, t01)]
        return add(*terms) * factor

    weight_grad = by_core(core, rows_of(core), to_core(rows_of(1 - core)), 1)[None]
    return (input_grad, weight_grad, new_outer, new_momentum, new_inner)


def solution(mesh):
    return jax.shard_map(
        shards,
        mesh=mesh,
        in_specs=(
            P(("replica", "shard"), None),
            P(("replica", "shard"), None),
            P("replica", "shard", None),
            P("replica", "shard", None),
            P("shard", None),
            P("shard", "replica"),
        ),
        out_specs=(
            P(("replica", "shard"), None),
            P("replica", "shard", None),
            P("shard", "replica"),
            P("shard", "replica"),
            P("shard", None),
        ),
        check_vma=False,
    )
```

```python
import functools

import jax
import jax.numpy as jnp
from jax import lax
from jax.experimental import pallas as pl
from jax.experimental.pallas import tpu as pltpu
from jax.sharding import PartitionSpec as P

F32 = jnp.float32
BF16 = jnp.bfloat16
MIB = 1 << 20
COST = 0.3

NZ, NY, NC, NX, NL = 4, 2, 2, 4, 2
DIRS = [(dz, dy) for dz in range(NZ) for dy in range(NY)]


def shard_perm(dz, dy, dc):
    perm = []
    for i in range(NZ * NY * NC):
        z, y, c = i // (NY * NC), (i // NC) % NY, i % NC
        j = ((z + dz) % NZ) * NY * NC + ((y + dy) % NY) * NC + (c + dc) % NC
        perm.append((i, j))
    return perm


def to_zp(a):
    return lax.ppermute(a, "shard", shard_perm(1, 0, 0))


def to_zm(a):
    return lax.ppermute(a, "shard", shard_perm(-1, 0, 0))


def to_y(a):
    return lax.ppermute(a, "shard", shard_perm(0, 1, 0))


def to_core(a):
    return lax.ppermute(a, "shard", shard_perm(0, 0, 1))


def to_l(a):
    return lax.ppermute(a, "replica", [(i, i ^ 1) for i in range(NX * NL)])


def to_x(a, dx):
    perm = [(i, (i // NL + dx) % NX * NL + i % NL) for i in range(NX * NL)]
    return lax.ppermute(a, "replica", perm)


def to_l(a):
    return lax.ppermute(a, "replica", [(i, i ^ 1) for i in range(NX * NL)])


def to_near(a):
    return lax.ppermute(a, "replica", [(i, i ^ NL) for i in range(NX * NL)])


def to_far(a):
    perm = [(i, (NX - 1 - i // NL) * NL + i % NL) for i in range(NX * NL)]
    return lax.ppermute(a, "replica", perm)


def add(*terms):
    total = terms[0].astype(F32)
    for term in terms[1:]:
        total = total + term.astype(F32)
    return total


EARLY = [(3, 1), (1, 1), (2, 1)]
LATE = [(2, 0), (0, 1)]
LAST = [(3, 0), (1, 0), (0, 0)]
AT_EARLY = len(DIRS)
AT_LATE = AT_EARLY + len(EARLY)
AT_LAST = AT_LATE + len(LATE)
AT_CORE = AT_LAST + len(LAST)
AT_OTHER = AT_CORE + 1
AT_X = AT_CORE + 2


def place_of(where, s, depth, rows):
    base = s[where[0]]
    return base if depth == rows else base * (rows // depth) + where[1]


def whole(shape):
    return pl.BlockSpec(shape, lambda i, *_: (0,) * len(shape))


def cost(flops, nbytes, trans=0):
    return pl.CostEstimate(
        flops=int(COST * flops), bytes_accessed=int(COST * nbytes), transcendentals=int(COST * trans)
    )


def params(mib):
    return pltpu.CompilerParams(vmem_limit_bytes=mib * MIB)


def decode_kernel(pos_ref, outer_ref, inner_ref, *out_refs):
    step = pl.program_id(0)
    width = outer_ref.shape[1]
    decoded = []
    for g in range(width // 128):
        cols = slice(g * 128, (g + 1) * 128)
        delta = outer_ref[:, cols] - inner_ref[0, :, cols]
        top = jnp.max(jnp.abs(delta), axis=1, keepdims=True) + 1e-06
        scale = top.astype(BF16).astype(F32)
        code = (delta / scale).astype(BF16).astype(F32)
        decoded.append((code * scale).astype(BF16))
    decoded = jnp.concatenate(decoded, axis=1)
    for k, out_ref in enumerate(out_refs):
        @pl.when(step == k)
        def _(out_ref=out_ref):
            out_ref[...] = decoded


def decode(pos, outer, inner):
    rows, cols = outer.shape
    width = cols // NX
    return pl.pallas_call(
        decode_kernel,
        grid_spec=pltpu.PrefetchScalarGridSpec(
            num_scalar_prefetch=1,
            grid=(NX,),
            in_specs=[
                pl.BlockSpec((rows, width), lambda i, p: (0, lax.rem(p[AT_X] + i, NX))),
                pl.BlockSpec((1, rows, width), lambda i, p: (0, 0, lax.rem(p[AT_X] + i, NX))),
            ],
            out_specs=[whole((rows, width))] * NX,
        ),
        out_shape=[jax.ShapeDtypeStruct((rows, width), BF16)] * NX,
        compiler_params=params(60),
        cost_estimate=cost(10 * rows * cols, 10 * rows * cols),
        name="decode",
    )(pos, outer, inner)


def sum_kernel(n, factor, blk_ref, *refs):
    total = refs[0][...].astype(F32)
    for ref in refs[1:n]:
        total = total + ref[...].astype(F32)
    if factor is not None:
        total = total * factor
    refs[n][...] = total.astype(refs[n].dtype)


def sum_of(pos, terms, rows, dtype, at=None, factor=None):
    width = terms[0].shape[1]
    n = len(terms)
    tile = rows // 2
    first = (lambda s: 0) if at is None else (lambda s: 2 * s[at])
    return pl.pallas_call(
        functools.partial(sum_kernel, n, factor),
        grid_spec=pltpu.PrefetchScalarGridSpec(
            num_scalar_prefetch=1,
            grid=(2,),
            in_specs=[pl.BlockSpec((tile, width), lambda i, s: (first(s) + i, 0))] * n,
            out_specs=pl.BlockSpec((tile, width), lambda i, s: (i, 0)),
        ),
        out_shape=jax.ShapeDtypeStruct((rows, width), dtype),
        compiler_params=params(60),
        cost_estimate=cost(n * rows * width, 2 * (n + 1) * rows * width),
        name="sum",
    )(pos, *terms)


def fold_kernel(up_ref, a_ref, low_ref, b_ref, up_out, low_out):
    up_out[...] = (up_ref[...].astype(F32) + a_ref[...].astype(F32)).astype(BF16)
    low_out[...] = (low_ref[...].astype(F32) + b_ref[...].astype(F32)).astype(BF16)


def fold(up, a, low, b):
    rows, width = a.shape
    block = (rows, width // 2)
    upper, lower = pl.BlockSpec(block, lambda i: (0, i)), pl.BlockSpec(block, lambda i: (1, i))
    return pl.pallas_call(
        fold_kernel,
        grid=(2,),
        in_specs=[upper, upper, lower, upper],
        out_specs=[upper, lower],
        out_shape=[jax.ShapeDtypeStruct(up.shape, BF16)] * 2,
        input_output_aliases={0: 0, 2: 1},
        compiler_params=params(60),
        cost_estimate=cost(2 * rows * width, 12 * rows * width),
        name="fold",
    )(up, a, low, b)


def halves_kernel(a_ref, b_ref, up_ref, low_ref):
    total = (a_ref[...].astype(F32) + b_ref[...].astype(F32)).astype(BF16)
    step = pl.program_id(0)

    @pl.when(step == 0)
    def _():
        up_ref[...] = total

    @pl.when(step == 1)
    def _():
        low_ref[...] = total


def halves_of(a, b):
    rows, width = a.shape[0] // 2, a.shape[1]
    return pl.pallas_call(
        halves_kernel,
        grid=(2,),
        in_specs=[pl.BlockSpec((rows, width), lambda i: (i, 0))] * 2,
        out_specs=[whole((rows, width))] * 2,
        out_shape=[jax.ShapeDtypeStruct((rows, width), BF16)] * 2,
        compiler_params=params(60),
        cost_estimate=cost(2 * rows * width, 12 * rows * width),
        name="halves",
    )(a, b)


def pre_kernel(factor, n, has_sum, last, off_ref, *refs):
    refs = list(refs)
    pieces = [refs.pop(0) for _ in range(n)]
    x_refs = [[refs.pop(0) for _ in range(n)] for _ in range(2)]
    sums = [refs.pop(0) for _ in range(2)] if has_sum else [None, None]
    cots = [refs.pop(0) for _ in range(2)] if last else [None, None]
    for xs, sum_ref, cot_ref, out_ref in zip(x_refs, sums, cots, refs):
        pre = sum_ref[...] if has_sum else None
        for x_ref, piece in zip(xs, pieces):
            term = jnp.dot(x_ref[...], piece[...], preferred_element_type=F32)
            pre = term if pre is None else pre + term
        if last:
            pre = pre * factor
            sig = 0.5 + 0.5 * jnp.tanh(0.5 * pre)
            pre = (cot_ref[...].astype(F32) * sig * (1.0 + pre * (1.0 - sig))).astype(BF16)
        out_ref[...] = pre


def pre_of(factor, pos, x_pair, pieces, offs, sums=None, cots=None):
    toks, feats = x_pair[0].shape
    width = pieces[0].shape[1]
    depth = sum(p.shape[0] for p in pieces)
    tile = toks // 2
    n = len(pieces)
    rows = feats // (NZ * NY)
    row = pl.BlockSpec((tile, width), lambda i, s: (i, 0))
    x_specs = [
        pl.BlockSpec(
            (tile, p.shape[0]), lambda i, s, p=p, w=w: (i, place_of(w, s, p.shape[0], rows))
        )
        for p, w in zip(pieces, offs)
    ]
    in_specs = [whole(p.shape) for p in pieces] + x_specs + x_specs
    args = list(pieces) + [x_pair[0]] * n + [x_pair[1]] * n
    if sums is not None:
        in_specs += [row, row]
        args += list(sums)
    if cots is not None:
        in_specs += [pl.BlockSpec((tile, width), lambda i, s: (i, s[AT_CORE]))] * 2
        args += list(cots)
    last = cots is not None
    return pl.pallas_call(
        functools.partial(pre_kernel, factor, n, sums is not None, last),
        grid_spec=pltpu.PrefetchScalarGridSpec(
            num_scalar_prefetch=1,
            grid=(toks // tile,),
            in_specs=in_specs,
            out_specs=[row, row],
        ),
        out_shape=[jax.ShapeDtypeStruct((toks, width), BF16 if last else F32)] * 2,
        compiler_params=params(60),
        cost_estimate=cost(4 * toks * depth * width, 4 * toks * depth + 2 * depth * width + 8 * toks * width),
        name="slope" if last else "pre",
    )(pos, *args)


def wgrad_kernel(halves, blk_ref, xo_ref, xp_ref, so_ref, sp_ref, *out_refs):
    step = pl.program_id(0)
    dims = (((0,), (0,)), ((), ()))
    term = lax.dot_general(xo_ref[...], so_ref[...], dims, preferred_element_type=F32)
    term = term + lax.dot_general(xp_ref[...], sp_ref[...], dims, preferred_element_type=F32)
    term = term.astype(BF16)
    out_refs = list(out_refs)
    for k, halved in enumerate(halves):
        mine = [out_refs.pop(0) for _ in range(2 if halved else 1)]

        @pl.when(step == k)
        def _(mine=mine):
            at = 0
            for ref in mine:
                ref[...] = term[at:at + ref.shape[0]]
                at += ref.shape[0]


def wgrad_of(pos, at, halves, x_pair, slopes):
    toks, feats = x_pair[0].shape
    width = slopes[0].shape[1]
    n = len(halves)
    rows = feats // (NZ * NY)
    shapes = []
    for halved in halves:
        shapes += [(rows // 2, width)] * 2 if halved else [(rows, width)]
    outs = pl.pallas_call(
        functools.partial(wgrad_kernel, halves),
        grid_spec=pltpu.PrefetchScalarGridSpec(
            num_scalar_prefetch=1,
            grid=(n,),
            in_specs=[pl.BlockSpec((toks, rows), lambda i, s: (0, s[at + i]))] * 2
            + [whole((toks, width))] * 2,
            out_specs=[whole(s) for s in shapes],
        ),
        out_shape=[jax.ShapeDtypeStruct(s, BF16) for s in shapes],
        compiler_params=params(60),
        cost_estimate=cost(4 * toks * n * rows * width, 4 * toks * n * rows + 2 * n * rows * width),
        name="wgrad",
    )(pos, *x_pair, *slopes)
    outs = list(outs)
    return [[outs.pop(0) for _ in range(2)] if halved else outs.pop(0) for halved in halves]


def late_kernel(n, offs, rows, s_ref, xo_ref, xp_ref, so_ref, sp_ref, *refs):
    step = pl.program_id(0)
    m = len(offs)
    pieces, outs, part_ref = refs[:m], refs[m:m + n], refs[m + n]
    tile = part_ref.shape[0]

    @pl.when(step < n)
    def _():
        dims = (((0,), (0,)), ((), ()))
        term = lax.dot_general(xo_ref[...], so_ref[...], dims, preferred_element_type=F32)
        term = term + lax.dot_general(xp_ref[...], sp_ref[...], dims, preferred_element_type=F32)
        term = term.astype(BF16)
        for k, out_ref in enumerate(outs):
            @pl.when(step == k)
            def _(out_ref=out_ref):
                out_ref[...] = term

    @pl.when(step >= n)
    def _():
        dims = (((1,), (1,)), ((), ()))
        slope = sp_ref[pl.ds(pl.multiple_of((step - n) * tile, tile), tile), :]
        for where, piece in zip(offs, pieces):
            depth = piece.shape[0]
            cols = pl.ds(pl.multiple_of(place_of(where, s_ref, depth, rows) * depth, 256), depth)
            part_ref[:, cols] = lax.dot_general(
                slope, piece[...], dims, preferred_element_type=F32
            ).astype(BF16)


def late_of(pos, x_pair, slopes, offs, pieces):
    toks, feats = x_pair[0].shape
    width = slopes[0].shape[1]
    n = len(LATE)
    rows = feats // (NZ * NY)
    tile = toks // 2
    outs = pl.pallas_call(
        functools.partial(late_kernel, n, offs, rows),
        grid_spec=pltpu.PrefetchScalarGridSpec(
            num_scalar_prefetch=1,
            grid=(n + toks // tile,),
            in_specs=[pl.BlockSpec((toks, rows), lambda i, s: (0, s[AT_LATE + jnp.minimum(i, n - 1)]))] * 2
            + [whole((toks, width))] * 2
            + [whole(p.shape) for p in pieces],
            out_specs=[whole((rows, width))] * n
            + [pl.BlockSpec((tile, feats), lambda i, s: (jnp.maximum(i - n, 0), 0))],
        ),
        out_shape=[jax.ShapeDtypeStruct((rows, width), BF16)] * n
        + [jax.ShapeDtypeStruct((toks, feats), BF16)],
        compiler_params=params(60),
        cost_estimate=cost(
            2 * toks * (2 * n * rows + feats) * width, 4 * toks * feats + 4 * feats * width
        ),
        name="late",
    )(pos, *x_pair, *slopes, *pieces)
    return outs


def igrad_kernel(factor, offs, rows, has_term, pos_ref, s_ref, *refs):
    n = len(offs)
    out_ref = refs[-1]
    dims = (((1,), (1,)), ((), ()))
    for where, piece in zip(offs, refs):
        depth = piece.shape[0]
        cols = pl.ds(pl.multiple_of(place_of(where, pos_ref, depth, rows) * depth, 256), depth)
        total = lax.dot_general(s_ref[...], piece[...], dims, preferred_element_type=F32)
        if has_term:
            total = (total + refs[n][:, cols].astype(F32)) * factor
        out_ref[:, cols] = total.astype(BF16)


def igrad_of(factor, pos, offs, slope, pieces, term=None):
    toks, width = slope.shape
    feats = sum(p.shape[0] for p in pieces)
    tile = toks // 2
    extra = [] if term is None else [term]
    return pl.pallas_call(
        functools.partial(
            igrad_kernel, factor, offs, feats // (NZ * NY), term is not None
        ),
        grid_spec=pltpu.PrefetchScalarGridSpec(
            num_scalar_prefetch=1,
            grid=(toks // tile,),
            in_specs=[pl.BlockSpec((tile, width), lambda i, s: (i, 0))]
            + [whole(p.shape) for p in pieces]
            + [pl.BlockSpec((tile, feats), lambda i, s: (i, 0)) for _ in extra],
            out_specs=pl.BlockSpec((tile, feats), lambda i, s: (i, 0)),
        ),
        out_shape=jax.ShapeDtypeStruct((toks, feats), BF16),
        compiler_params=params(60),
        cost_estimate=cost(2 * toks * feats * width, 2 * toks * feats + 2 * feats * width),
        name="igrad",
    )(pos, slope, *pieces, *extra)


def by_core(core, mine, other, axis):
    return jnp.where(
        core == 0,
        jnp.concatenate([mine, other], axis=axis),
        jnp.concatenate([other, mine], axis=axis),
    )


def place_kernel(pos_ref, *refs):
    for k, part_ref in enumerate(refs[:-1]):
        @pl.when(pl.program_id(0) == k)
        def _(part_ref=part_ref):
            refs[-1][...] = part_ref[...]


def side_by_side(pos, parts):
    rows, width = parts[0].shape
    n = len(parts)
    return pl.pallas_call(
        place_kernel,
        grid_spec=pltpu.PrefetchScalarGridSpec(
            num_scalar_prefetch=1,
            grid=(n,),
            in_specs=[whole((rows, width))] * n,
            out_specs=pl.BlockSpec((rows, width), lambda i, p: (0, lax.rem(p[AT_X] + n - i, n))),
        ),
        out_shape=jax.ShapeDtypeStruct((rows, n * width), parts[0].dtype),
        compiler_params=params(60),
        cost_estimate=cost(0, 4 * n * rows * width),
        name="place",
    )(pos, *parts)


def hold(a, *deps):
    return lax.optimization_barrier((a,) + deps)[0]


def shards(tokens, cotangent, next_weight, inner_weight, outer_weight, momentum):
    toks, feats = tokens.shape
    factor = feats ** (-0.5)
    me = lax.axis_index("shard")
    z, y, core = me // (NY * NC), (me // NC) % NY, me % NC
    replica = lax.axis_index("replica")
    low = replica % NL

    blk = {(dz, dy): ((z + dz) % NZ) * NY + (y + dy) % NY for dz, dy in DIRS}
    rows = feats // (NZ * NY)
    half = rows // 2
    cols = next_weight.shape[2] // NC

    def offs(*dirs):
        return [(DIRS.index(d[:2]), d[2] if len(d) == 3 else 0) for d in dirs]

    pos = jnp.stack(
        [blk[d] for d in DIRS + EARLY + LATE + LAST] + [core, 1 - core, replica // NL]
    ).astype(jnp.int32)

    keep = lax.dynamic_slice_in_dim(next_weight[0], core * cols, cols, 1)
    give = lax.dynamic_slice_in_dim(next_weight[0], (1 - core) * cols, cols, 1)
    w00 = by_core(core, keep, to_core(give), 0)

    w30, w10, w01 = to_zp(w00), to_zm(w00), to_y(w00)
    x_pair = (tokens, to_core(hold(tokens, w00)))
    cots = (cotangent, to_core(hold(cotangent, w00)))
    dec = decode(pos, hold(outer_weight, w00), inner_weight)
    x1, x2, x3 = [to_x(hold(dec[dx], x_pair[1], cots[1]), dx) for dx in (1, 2, 3)]

    a20 = to_zp(hold(w30, w01, dec[0], x1)[:half])
    b20 = to_zm(hold(w10, w01, dec[0], x1)[half:])
    first, first_offs = [w00, w30, w10, w01], offs((0, 0), (3, 0), (1, 0), (0, 1))
    sums = pre_of(factor, pos, x_pair, first, first_offs)

    a21, b21 = to_y(hold(a20, sums[0])), to_y(hold(b20, sums[0]))
    w31, w11 = to_zp(hold(w01, sums[0], a20)), to_zm(hold(w01, sums[0], b20))
    share = momentum.shape[1]

    def share_of(a, which):
        return lax.dynamic_slice_in_dim(a, which * share, share, 1)

    second, second_offs = [a20, b20], offs((2, 0), (2, 0, 1))
    sums = pre_of(factor, pos, x_pair, second, second_offs, sums)
    x_terms = [hold(dec[0], sums[0]), x1, x2, x3]
    other = add(*[share_of(a, 1 - low) for a in x_terms]).astype(BF16)
    low_got = to_l(hold(other, a21, b21, w31, w11))
    third, third_offs = [w31, w11, a21, b21], offs((3, 1), (1, 1), (2, 1), (2, 1, 1))
    slopes = pre_of(factor, pos, x_pair, third, third_offs, sums, cots)
    mine = [share_of(a, low) for a in x_terms]
    average = add(*mine, hold(low_got, slopes[0])) / (NX * NL)
    outer_share = lax.dynamic_slice_in_dim(outer_weight, replica * share, share, 1)
    new_momentum = 0.9 * momentum + average
    new_outer = outer_share - 0.7 * (average + 0.9 * new_momentum)
    inner_share = new_outer.astype(BF16)
    inner_other = to_l(inner_share)

    early_slopes = (hold(slopes[0], inner_share), slopes[1])
    g31, g11, g21 = wgrad_of(pos, AT_EARLY, (False,) * 3, x_pair, early_slopes)
    inner_other = hold(inner_other, g21)
    inner_pair = by_core(low, inner_share, inner_other, 1)
    g31, g11, g21 = [hold(g, inner_other) for g in (g31, g11, g21)]
    e2 = to_x(inner_pair, 2)

    r31, r11, r21 = to_zm(g31), to_zp(g11), to_y(g21)
    late_slopes = (hold(slopes[0], inner_pair), slopes[1])
    pieces, piece_offs = first + second + third, first_offs + second_offs + third_offs
    g20, g01, part = late_of(pos, x_pair, late_slopes, piece_offs, pieces)

    ha20, hb20 = halves_of(g20, hold(r21, r31, r11, e2))
    ra20, rb20 = to_zm(ha20), to_zp(hb20)
    part_got = to_core(hold(part, ha20))
    last_slopes = (hold(slopes[0], ha20, hb20), slopes[1])
    g30, g10, g00 = wgrad_of(pos, AT_LAST, (False,) * 3, x_pair, last_slopes)
    s01 = sum_of(pos, [g01, hold(r31, g30), r11], rows, BF16)
    t01 = to_y(s01)

    s30, s10 = fold(g30, ra20, g10, hold(rb20, s01))
    t30, t10 = to_zm(s30), to_zp(s10)
    e1, e3 = [to_x(hold(inner_pair, s30), dx) for dx in (1, 3)]
    input_grad = igrad_of(
        factor, pos, piece_offs, hold(slopes[0], s30, s10), pieces, part_got
    )
    new_inner = side_by_side(pos, [hold(inner_pair, input_grad), e1, e2, e3])
    terms = [hold(g00, new_inner), t30, t10, t01]

    def rows_of(which, own):
        halves = [lax.dynamic_slice_in_dim(a, which * half, half, 0) for a in [own] + terms[1:]]
        return add(*halves) * factor

    give_rows = rows_of(1 - core, terms[0])
    keep_rows = rows_of(core, hold(terms[0], give_rows))
    weight_grad = by_core(core, keep_rows, to_core(give_rows), 1)[None]
    return (input_grad, weight_grad, new_outer, new_momentum, new_inner)


def solution(mesh):
    return jax.shard_map(
        shards,
        mesh=mesh,
        in_specs=(
            P(("replica", "shard"), None),
            P(("replica", "shard"), None),
            P("replica", "shard", None),
            P("replica", "shard", None),
            P("shard", None),
            P("shard", "replica"),
        ),
        out_specs=(
            P(("replica", "shard"), None),
            P("replica", "shard", None),
            P("shard", "replica"),
            P("shard", "replica"),
            P("shard", None),
        ),
        check_vma=False,
    )
```

```python
import functools

import jax
import jax.numpy as jnp
from jax import lax
from jax.experimental import pallas as pl
from jax.experimental.pallas import tpu as pltpu
from jax.sharding import PartitionSpec as P

F32 = jnp.float32
BF16 = jnp.bfloat16
MIB = 1 << 20
COST = 0.3

NZ, NY, NC, NX, NL = 4, 2, 2, 4, 2
DIRS = [(dz, dy) for dz in range(NZ) for dy in range(NY)]


def shard_perm(dz, dy, dc):
    perm = []
    for i in range(NZ * NY * NC):
        z, y, c = i // (NY * NC), (i // NC) % NY, i % NC
        j = ((z + dz) % NZ) * NY * NC + ((y + dy) % NY) * NC + (c + dc) % NC
        perm.append((i, j))
    return perm


def to_zp(a):
    return lax.ppermute(a, "shard", shard_perm(1, 0, 0))


def to_zm(a):
    return lax.ppermute(a, "shard", shard_perm(-1, 0, 0))


def to_y(a):
    return lax.ppermute(a, "shard", shard_perm(0, 1, 0))


def to_core(a):
    return lax.ppermute(a, "shard", shard_perm(0, 0, 1))


def to_l(a):
    return lax.ppermute(a, "replica", [(i, i ^ 1) for i in range(NX * NL)])


def to_x(a, dx):
    perm = [(i, (i // NL + dx) % NX * NL + i % NL) for i in range(NX * NL)]
    return lax.ppermute(a, "replica", perm)


def to_l(a):
    return lax.ppermute(a, "replica", [(i, i ^ 1) for i in range(NX * NL)])


def to_near(a):
    return lax.ppermute(a, "replica", [(i, i ^ NL) for i in range(NX * NL)])


def to_far(a):
    perm = [(i, (NX - 1 - i // NL) * NL + i % NL) for i in range(NX * NL)]
    return lax.ppermute(a, "replica", perm)


def add(*terms):
    total = terms[0].astype(F32)
    for term in terms[1:]:
        total = total + term.astype(F32)
    return total


EARLY = [(3, 1), (1, 1), (2, 1)]
LATE = [(2, 0), (0, 1), (0, 0)]
LAST = [(3, 0), (1, 0)]
AT_EARLY = len(DIRS)
AT_LATE = AT_EARLY + len(EARLY)
AT_LAST = AT_LATE + len(LATE)
AT_CORE = AT_LAST + len(LAST)
AT_OTHER = AT_CORE + 1
AT_X = AT_CORE + 2


def place_of(where, s, depth, rows):
    base = s[where[0]]
    return base if depth == rows else base * (rows // depth) + where[1]


def whole(shape):
    return pl.BlockSpec(shape, lambda i, *_: (0,) * len(shape))


def cost(flops, nbytes, trans=0):
    return pl.CostEstimate(
        flops=int(COST * flops), bytes_accessed=int(COST * nbytes), transcendentals=int(COST * trans)
    )


def params(mib):
    return pltpu.CompilerParams(vmem_limit_bytes=mib * MIB)


def decode_kernel(pos_ref, outer_ref, inner_ref, *out_refs):
    step = pl.program_id(0)
    width = outer_ref.shape[1]
    decoded = []
    for g in range(width // 128):
        cols = slice(g * 128, (g + 1) * 128)
        delta = outer_ref[:, cols] - inner_ref[0, :, cols]
        top = jnp.max(jnp.abs(delta), axis=1, keepdims=True) + 1e-06
        scale = top.astype(BF16).astype(F32)
        code = (delta / scale).astype(BF16).astype(F32)
        decoded.append((code * scale).astype(BF16))
    decoded = jnp.concatenate(decoded, axis=1)
    for k, out_ref in enumerate(out_refs):
        @pl.when(step == k)
        def _(out_ref=out_ref):
            out_ref[...] = decoded


def decode(pos, outer, inner):
    rows, cols = outer.shape
    width = cols // NX
    return pl.pallas_call(
        decode_kernel,
        grid_spec=pltpu.PrefetchScalarGridSpec(
            num_scalar_prefetch=1,
            grid=(NX,),
            in_specs=[
                pl.BlockSpec((rows, width), lambda i, p: (0, lax.rem(p[AT_X] + i, NX))),
                pl.BlockSpec((1, rows, width), lambda i, p: (0, 0, lax.rem(p[AT_X] + i, NX))),
            ],
            out_specs=[whole((rows, width))] * NX,
        ),
        out_shape=[jax.ShapeDtypeStruct((rows, width), BF16)] * NX,
        compiler_params=params(60),
        cost_estimate=cost(10 * rows * cols, 10 * rows * cols),
        name="decode",
    )(pos, outer, inner)


def sum_kernel(n, factor, blk_ref, *refs):
    total = refs[0][...].astype(F32)
    for ref in refs[1:n]:
        total = total + ref[...].astype(F32)
    if factor is not None:
        total = total * factor
    refs[n][...] = total.astype(refs[n].dtype)


def sum_of(pos, terms, rows, dtype, at=None, factor=None):
    width = terms[0].shape[1]
    n = len(terms)
    tile = rows // 2
    first = (lambda s: 0) if at is None else (lambda s: 2 * s[at])
    return pl.pallas_call(
        functools.partial(sum_kernel, n, factor),
        grid_spec=pltpu.PrefetchScalarGridSpec(
            num_scalar_prefetch=1,
            grid=(2,),
            in_specs=[pl.BlockSpec((tile, width), lambda i, s: (first(s) + i, 0))] * n,
            out_specs=pl.BlockSpec((tile, width), lambda i, s: (i, 0)),
        ),
        out_shape=jax.ShapeDtypeStruct((rows, width), dtype),
        compiler_params=params(60),
        cost_estimate=cost(n * rows * width, 2 * (n + 1) * rows * width),
        name="sum",
    )(pos, *terms)


def fold_kernel(up_ref, a_ref, low_ref, b_ref, up_out, low_out):
    up_out[...] = (up_ref[...].astype(F32) + a_ref[...].astype(F32)).astype(BF16)
    low_out[...] = (low_ref[...].astype(F32) + b_ref[...].astype(F32)).astype(BF16)


def fold(up, a, low, b):
    rows, width = a.shape
    block = (rows, width // 2)
    upper, lower = pl.BlockSpec(block, lambda i: (0, i)), pl.BlockSpec(block, lambda i: (1, i))
    return pl.pallas_call(
        fold_kernel,
        grid=(2,),
        in_specs=[upper, upper, lower, upper],
        out_specs=[upper, lower],
        out_shape=[jax.ShapeDtypeStruct(up.shape, BF16)] * 2,
        input_output_aliases={0: 0, 2: 1},
        compiler_params=params(60),
        cost_estimate=cost(2 * rows * width, 12 * rows * width),
        name="fold",
    )(up, a, low, b)


def halves_kernel(a_ref, b_ref, up_ref, low_ref):
    total = (a_ref[...].astype(F32) + b_ref[...].astype(F32)).astype(BF16)
    step = pl.program_id(0)

    @pl.when(step == 0)
    def _():
        up_ref[...] = total

    @pl.when(step == 1)
    def _():
        low_ref[...] = total


def halves_of(a, b):
    rows, width = a.shape[0] // 2, a.shape[1]
    return pl.pallas_call(
        halves_kernel,
        grid=(2,),
        in_specs=[pl.BlockSpec((rows, width), lambda i: (i, 0))] * 2,
        out_specs=[whole((rows, width))] * 2,
        out_shape=[jax.ShapeDtypeStruct((rows, width), BF16)] * 2,
        compiler_params=params(60),
        cost_estimate=cost(2 * rows * width, 12 * rows * width),
        name="halves",
    )(a, b)


def pre_kernel(factor, n, has_sum, last, off_ref, *refs):
    refs = list(refs)
    pieces = [refs.pop(0) for _ in range(n)]
    x_refs = [[refs.pop(0) for _ in range(n)] for _ in range(2)]
    sums = [refs.pop(0) for _ in range(2)] if has_sum else [None, None]
    cots = [refs.pop(0) for _ in range(2)] if last else [None, None]
    for xs, sum_ref, cot_ref, out_ref in zip(x_refs, sums, cots, refs):
        pre = sum_ref[...] if has_sum else None
        for x_ref, piece in zip(xs, pieces):
            term = jnp.dot(x_ref[...], piece[...], preferred_element_type=F32)
            pre = term if pre is None else pre + term
        if last:
            pre = pre * factor
            sig = 0.5 + 0.5 * jnp.tanh(0.5 * pre)
            pre = (cot_ref[...].astype(F32) * sig * (1.0 + pre * (1.0 - sig))).astype(BF16)
        out_ref[...] = pre


def pre_of(factor, pos, x_pair, pieces, offs, sums=None, cots=None):
    toks, feats = x_pair[0].shape
    width = pieces[0].shape[1]
    depth = sum(p.shape[0] for p in pieces)
    tile = toks // 2
    n = len(pieces)
    rows = feats // (NZ * NY)
    row = pl.BlockSpec((tile, width), lambda i, s: (i, 0))
    x_specs = [
        pl.BlockSpec(
            (tile, p.shape[0]), lambda i, s, p=p, w=w: (i, place_of(w, s, p.shape[0], rows))
        )
        for p, w in zip(pieces, offs)
    ]
    in_specs = [whole(p.shape) for p in pieces] + x_specs + x_specs
    args = list(pieces) + [x_pair[0]] * n + [x_pair[1]] * n
    if sums is not None:
        in_specs += [row, row]
        args += list(sums)
    if cots is not None:
        in_specs += [pl.BlockSpec((tile, width), lambda i, s: (i, s[AT_CORE]))] * 2
        args += list(cots)
    last = cots is not None
    return pl.pallas_call(
        functools.partial(pre_kernel, factor, n, sums is not None, last),
        grid_spec=pltpu.PrefetchScalarGridSpec(
            num_scalar_prefetch=1,
            grid=(toks // tile,),
            in_specs=in_specs,
            out_specs=[row, row],
        ),
        out_shape=[jax.ShapeDtypeStruct((toks, width), BF16 if last else F32)] * 2,
        compiler_params=params(60),
        cost_estimate=cost(4 * toks * depth * width, 4 * toks * depth + 2 * depth * width + 8 * toks * width),
        name="slope" if last else "pre",
    )(pos, *args)


def wgrad_kernel(halves, blk_ref, xo_ref, xp_ref, so_ref, sp_ref, *out_refs):
    step = pl.program_id(0)
    dims = (((0,), (0,)), ((), ()))
    term = lax.dot_general(xo_ref[...], so_ref[...], dims, preferred_element_type=F32)
    term = term + lax.dot_general(xp_ref[...], sp_ref[...], dims, preferred_element_type=F32)
    term = term.astype(BF16)
    out_refs = list(out_refs)
    for k, halved in enumerate(halves):
        mine = [out_refs.pop(0) for _ in range(2 if halved else 1)]

        @pl.when(step == k)
        def _(mine=mine):
            at = 0
            for ref in mine:
                ref[...] = term[at:at + ref.shape[0]]
                at += ref.shape[0]


def wgrad_of(pos, at, halves, x_pair, slopes):
    toks, feats = x_pair[0].shape
    width = slopes[0].shape[1]
    n = len(halves)
    rows = feats // (NZ * NY)
    shapes = []
    for halved in halves:
        shapes += [(rows // 2, width)] * 2 if halved else [(rows, width)]
    outs = pl.pallas_call(
        functools.partial(wgrad_kernel, halves),
        grid_spec=pltpu.PrefetchScalarGridSpec(
            num_scalar_prefetch=1,
            grid=(n,),
            in_specs=[pl.BlockSpec((toks, rows), lambda i, s: (0, s[at + i]))] * 2
            + [whole((toks, width))] * 2,
            out_specs=[whole(s) for s in shapes],
        ),
        out_shape=[jax.ShapeDtypeStruct(s, BF16) for s in shapes],
        compiler_params=params(60),
        cost_estimate=cost(4 * toks * n * rows * width, 4 * toks * n * rows + 2 * n * rows * width),
        name="wgrad",
    )(pos, *x_pair, *slopes)
    outs = list(outs)
    return [[outs.pop(0) for _ in range(2)] if halved else outs.pop(0) for halved in halves]


def late_kernel(n, offs, rows, s_ref, xo_ref, xp_ref, so_ref, sp_ref, *refs):
    step = pl.program_id(0)
    m = len(offs)
    pieces, outs, part_ref = refs[:m], refs[m:m + n], refs[m + n]
    tile = part_ref.shape[0]

    @pl.when(step < n)
    def _():
        dims = (((0,), (0,)), ((), ()))
        term = lax.dot_general(xo_ref[...], so_ref[...], dims, preferred_element_type=F32)
        term = term + lax.dot_general(xp_ref[...], sp_ref[...], dims, preferred_element_type=F32)
        term = term.astype(BF16)
        for k, out_ref in enumerate(outs):
            @pl.when(step == k)
            def _(out_ref=out_ref):
                out_ref[...] = term

    @pl.when(step >= n)
    def _():
        dims = (((1,), (1,)), ((), ()))
        slope = sp_ref[pl.ds(pl.multiple_of((step - n) * tile, tile), tile), :]
        for where, piece in zip(offs, pieces):
            depth = piece.shape[0]
            cols = pl.ds(pl.multiple_of(place_of(where, s_ref, depth, rows) * depth, 256), depth)
            part_ref[:, cols] = lax.dot_general(
                slope, piece[...], dims, preferred_element_type=F32
            ).astype(BF16)


def late_of(pos, x_pair, slopes, offs, pieces):
    toks, feats = x_pair[0].shape
    width = slopes[0].shape[1]
    n = len(LATE)
    rows = feats // (NZ * NY)
    tile = toks // 2
    outs = pl.pallas_call(
        functools.partial(late_kernel, n, offs, rows),
        grid_spec=pltpu.PrefetchScalarGridSpec(
            num_scalar_prefetch=1,
            grid=(n + toks // tile,),
            in_specs=[pl.BlockSpec((toks, rows), lambda i, s: (0, s[AT_LATE + jnp.minimum(i, n - 1)]))] * 2
            + [whole((toks, width))] * 2
            + [whole(p.shape) for p in pieces],
            out_specs=[whole((rows, width))] * n
            + [pl.BlockSpec((tile, feats), lambda i, s: (jnp.maximum(i - n, 0), 0))],
        ),
        out_shape=[jax.ShapeDtypeStruct((rows, width), BF16)] * n
        + [jax.ShapeDtypeStruct((toks, feats), BF16)],
        compiler_params=params(60),
        cost_estimate=cost(
            2 * toks * (2 * n * rows + feats) * width, 4 * toks * feats + 4 * feats * width
        ),
        name="late",
    )(pos, *x_pair, *slopes, *pieces)
    return outs


def igrad_kernel(factor, offs, rows, has_term, pos_ref, s_ref, *refs):
    n = len(offs)
    out_ref = refs[-1]
    dims = (((1,), (1,)), ((), ()))
    for where, piece in zip(offs, refs):
        depth = piece.shape[0]
        cols = pl.ds(pl.multiple_of(place_of(where, pos_ref, depth, rows) * depth, 256), depth)
        total = lax.dot_general(s_ref[...], piece[...], dims, preferred_element_type=F32)
        if has_term:
            total = (total + refs[n][:, cols].astype(F32)) * factor
        out_ref[:, cols] = total.astype(BF16)


def igrad_of(factor, pos, offs, slope, pieces, term=None):
    toks, width = slope.shape
    feats = sum(p.shape[0] for p in pieces)
    tile = toks // 2
    extra = [] if term is None else [term]
    return pl.pallas_call(
        functools.partial(
            igrad_kernel, factor, offs, feats // (NZ * NY), term is not None
        ),
        grid_spec=pltpu.PrefetchScalarGridSpec(
            num_scalar_prefetch=1,
            grid=(toks // tile,),
            in_specs=[pl.BlockSpec((tile, width), lambda i, s: (i, 0))]
            + [whole(p.shape) for p in pieces]
            + [pl.BlockSpec((tile, feats), lambda i, s: (i, 0)) for _ in extra],
            out_specs=pl.BlockSpec((tile, feats), lambda i, s: (i, 0)),
        ),
        out_shape=jax.ShapeDtypeStruct((toks, feats), BF16),
        compiler_params=params(60),
        cost_estimate=cost(2 * toks * feats * width, 2 * toks * feats + 2 * feats * width),
        name="igrad",
    )(pos, slope, *pieces, *extra)


def by_core(core, mine, other, axis):
    return jnp.where(
        core == 0,
        jnp.concatenate([mine, other], axis=axis),
        jnp.concatenate([other, mine], axis=axis),
    )


def place_kernel(pos_ref, *refs):
    for k, part_ref in enumerate(refs[:-1]):
        @pl.when(pl.program_id(0) == k)
        def _(part_ref=part_ref):
            refs[-1][...] = part_ref[...]


def side_by_side(pos, parts):
    rows, width = parts[0].shape
    n = len(parts)
    return pl.pallas_call(
        place_kernel,
        grid_spec=pltpu.PrefetchScalarGridSpec(
            num_scalar_prefetch=1,
            grid=(n,),
            in_specs=[whole((rows, width))] * n,
            out_specs=pl.BlockSpec((rows, width), lambda i, p: (0, lax.rem(p[AT_X] + n - i, n))),
        ),
        out_shape=jax.ShapeDtypeStruct((rows, n * width), parts[0].dtype),
        compiler_params=params(60),
        cost_estimate=cost(0, 4 * n * rows * width),
        name="place",
    )(pos, *parts)


def hold(a, *deps):
    return lax.optimization_barrier((a,) + deps)[0]


def shards(tokens, cotangent, next_weight, inner_weight, outer_weight, momentum):
    toks, feats = tokens.shape
    factor = feats ** (-0.5)
    me = lax.axis_index("shard")
    z, y, core = me // (NY * NC), (me // NC) % NY, me % NC
    replica = lax.axis_index("replica")
    low = replica % NL

    blk = {(dz, dy): ((z + dz) % NZ) * NY + (y + dy) % NY for dz, dy in DIRS}
    rows = feats // (NZ * NY)
    half = rows // 2
    cols = next_weight.shape[2] // NC

    def offs(*dirs):
        return [(DIRS.index(d[:2]), d[2] if len(d) == 3 else 0) for d in dirs]

    pos = jnp.stack(
        [blk[d] for d in DIRS + EARLY + LATE + LAST] + [core, 1 - core, replica // NL]
    ).astype(jnp.int32)

    keep = lax.dynamic_slice_in_dim(next_weight[0], core * cols, cols, 1)
    give = lax.dynamic_slice_in_dim(next_weight[0], (1 - core) * cols, cols, 1)
    w00 = by_core(core, keep, to_core(give), 0)

    w30, w10, w01 = to_zp(w00), to_zm(w00), to_y(w00)
    x_pair = (tokens, to_core(hold(tokens, w00)))
    cots = (cotangent, to_core(hold(cotangent, w00)))
    dec = decode(pos, hold(outer_weight, w00), inner_weight)
    x1, x2, x3 = [to_x(hold(dec[dx], x_pair[1], cots[1]), dx) for dx in (1, 2, 3)]

    a20 = to_zp(hold(w30, w01, dec[0], x1)[:half])
    b20 = to_zm(hold(w10, w01, dec[0], x1)[half:])
    first, first_offs = [w00, w30, w10, w01], offs((0, 0), (3, 0), (1, 0), (0, 1))
    sums = pre_of(factor, pos, x_pair, first, first_offs)

    a21, b21 = to_y(hold(a20, sums[0])), to_y(hold(b20, sums[0]))
    w31, w11 = to_zp(hold(w01, sums[0], a20)), to_zm(hold(w01, sums[0], b20))
    share = momentum.shape[1]

    def share_of(a, which):
        return lax.dynamic_slice_in_dim(a, which * share, share, 1)

    second, second_offs = [a20, b20], offs((2, 0), (2, 0, 1))
    sums = pre_of(factor, pos, x_pair, second, second_offs, sums)
    x_terms = [hold(dec[0], sums[0]), x1, x2, x3]
    other = add(*[share_of(a, 1 - low) for a in x_terms]).astype(BF16)
    mine = add(*[share_of(a, low) for a in x_terms])
    outer_share = lax.dynamic_slice_in_dim(outer_weight, replica * share, share, 1)
    outer_share = hold(outer_share, sums[0])
    low_got = to_l(hold(other, mine, outer_share, a21, b21, w31, w11))
    third, third_offs = [w31, w11, a21, b21], offs((3, 1), (1, 1), (2, 1), (2, 1, 1))
    slopes = pre_of(factor, pos, x_pair, third, third_offs, sums, cots)
    average = (mine + hold(low_got, slopes[0]).astype(F32)) / (NX * NL)
    new_momentum = 0.9 * momentum + average
    new_outer = outer_share - 0.7 * (average + 0.9 * new_momentum)
    inner_share = new_outer.astype(BF16)
    inner_other = to_l(inner_share)

    early_slopes = (hold(slopes[0], inner_share), slopes[1])
    g31, g11, g21 = wgrad_of(pos, AT_EARLY, (False,) * 3, x_pair, early_slopes)
    inner_other = hold(inner_other, g21)
    inner_pair = by_core(low, inner_share, inner_other, 1)
    g31, g11, g21 = [hold(g, inner_other) for g in (g31, g11, g21)]
    e2 = to_x(inner_pair, 2)

    r31, r11, r21 = to_zm(g31), to_zp(g11), to_y(g21)
    late_slopes = (hold(slopes[0], inner_pair), slopes[1])
    pieces, piece_offs = first + second + third, first_offs + second_offs + third_offs
    g20, g01, g00, part = late_of(pos, x_pair, late_slopes, piece_offs, pieces)

    ha20, hb20 = halves_of(g20, hold(r21, r31, r11, e2))
    ra20, rb20 = to_zm(ha20), to_zp(hb20)
    part_got = to_core(hold(part, ha20))
    s01 = sum_of(pos, [g01, hold(r31, ha20, hb20), r11], rows, BF16)
    t01 = to_y(s01)
    last_slopes = (hold(slopes[0], ha20, hb20, s01), slopes[1])
    g30, g10 = wgrad_of(pos, AT_LAST, (False,) * 2, x_pair, last_slopes)

    s30, s10 = fold(g30, ra20, g10, rb20)
    t30, t10 = to_zm(s30), to_zp(s10)
    e1, e3 = [to_x(hold(inner_pair, s30), dx) for dx in (1, 3)]
    input_grad = igrad_of(
        factor, pos, piece_offs, hold(slopes[0], s30, s10), pieces, part_got
    )
    new_inner = side_by_side(pos, [hold(inner_pair, input_grad), e1, e2, e3])
    terms = [hold(g00, new_inner), t30, t10, t01]

    def rows_of(which, own):
        halves = [lax.dynamic_slice_in_dim(a, which * half, half, 0) for a in [own] + terms[1:]]
        return add(*halves) * factor

    give_rows = rows_of(1 - core, terms[0])
    keep_rows = rows_of(core, hold(terms[0], give_rows))
    weight_grad = by_core(core, keep_rows, to_core(give_rows), 1)[None]
    return (input_grad, weight_grad, new_outer, new_momentum, new_inner)


def solution(mesh):
    return jax.shard_map(
        shards,
        mesh=mesh,
        in_specs=(
            P(("replica", "shard"), None),
            P(("replica", "shard"), None),
            P("replica", "shard", None),
            P("replica", "shard", None),
            P("shard", None),
            P("shard", "replica"),
        ),
        out_specs=(
            P(("replica", "shard"), None),
            P("replica", "shard", None),
            P("shard", "replica"),
            P("shard", "replica"),
            P("shard", None),
        ),
        check_vma=False,
    )
```

```python
import functools

import jax
import jax.numpy as jnp
from jax import lax
from jax.experimental import pallas as pl
from jax.experimental.pallas import tpu as pltpu
from jax.sharding import PartitionSpec as P

F32 = jnp.float32
BF16 = jnp.bfloat16
MIB = 1 << 20
COST = 0.3

NZ, NY, NC, NX, NL = 4, 2, 2, 4, 2
DIRS = [(dz, dy) for dz in range(NZ) for dy in range(NY)]


def shard_perm(dz, dy, dc):
    perm = []
    for i in range(NZ * NY * NC):
        z, y, c = i // (NY * NC), (i // NC) % NY, i % NC
        j = ((z + dz) % NZ) * NY * NC + ((y + dy) % NY) * NC + (c + dc) % NC
        perm.append((i, j))
    return perm


def to_zp(a):
    return lax.ppermute(a, "shard", shard_perm(1, 0, 0))


def to_zm(a):
    return lax.ppermute(a, "shard", shard_perm(-1, 0, 0))


def to_y(a):
    return lax.ppermute(a, "shard", shard_perm(0, 1, 0))


def to_core(a):
    return lax.ppermute(a, "shard", shard_perm(0, 0, 1))


def to_l(a):
    return lax.ppermute(a, "replica", [(i, i ^ 1) for i in range(NX * NL)])


def to_x(a, dx):
    perm = [(i, (i // NL + dx) % NX * NL + i % NL) for i in range(NX * NL)]
    return lax.ppermute(a, "replica", perm)


def to_l(a):
    return lax.ppermute(a, "replica", [(i, i ^ 1) for i in range(NX * NL)])


def to_near(a):
    return lax.ppermute(a, "replica", [(i, i ^ NL) for i in range(NX * NL)])


def to_far(a):
    perm = [(i, (NX - 1 - i // NL) * NL + i % NL) for i in range(NX * NL)]
    return lax.ppermute(a, "replica", perm)


def add(*terms):
    total = terms[0].astype(F32)
    for term in terms[1:]:
        total = total + term.astype(F32)
    return total


EARLY = [(3, 1), (1, 1), (2, 1)]
LATE = [(2, 0), (0, 1), (0, 0)]
LAST = [(3, 0), (1, 0)]
AT_EARLY = len(DIRS)
AT_LATE = AT_EARLY + len(EARLY)
AT_LAST = AT_LATE + len(LATE)
AT_CORE = AT_LAST + len(LAST)
AT_OTHER = AT_CORE + 1
AT_X = AT_CORE + 2


def place_of(where, s, depth, rows):
    base = s[where[0]]
    return base if depth == rows else base * (rows // depth) + where[1]


def whole(shape):
    return pl.BlockSpec(shape, lambda i, *_: (0,) * len(shape))


def cost(flops, nbytes, trans=0):
    return pl.CostEstimate(
        flops=int(COST * flops), bytes_accessed=int(COST * nbytes), transcendentals=int(COST * trans)
    )


def params(mib):
    return pltpu.CompilerParams(vmem_limit_bytes=mib * MIB)


def decode_kernel(pos_ref, outer_ref, inner_ref, *out_refs):
    step = pl.program_id(0)
    width = outer_ref.shape[1]
    decoded = []
    for g in range(width // 128):
        cols = slice(g * 128, (g + 1) * 128)
        delta = outer_ref[:, cols] - inner_ref[0, :, cols]
        top = jnp.max(jnp.abs(delta), axis=1, keepdims=True) + 1e-06
        scale = top.astype(BF16).astype(F32)
        code = (delta / scale).astype(BF16).astype(F32)
        decoded.append((code * scale).astype(BF16))
    decoded = jnp.concatenate(decoded, axis=1)
    for k, out_ref in enumerate(out_refs):
        @pl.when(step == k)
        def _(out_ref=out_ref):
            out_ref[...] = decoded


def decode(pos, outer, inner):
    rows, cols = outer.shape
    width = cols // NX
    return pl.pallas_call(
        decode_kernel,
        grid_spec=pltpu.PrefetchScalarGridSpec(
            num_scalar_prefetch=1,
            grid=(NX,),
            in_specs=[
                pl.BlockSpec((rows, width), lambda i, p: (0, lax.rem(p[AT_X] + i, NX))),
                pl.BlockSpec((1, rows, width), lambda i, p: (0, 0, lax.rem(p[AT_X] + i, NX))),
            ],
            out_specs=[whole((rows, width))] * NX,
        ),
        out_shape=[jax.ShapeDtypeStruct((rows, width), BF16)] * NX,
        compiler_params=params(60),
        cost_estimate=cost(10 * rows * cols, 10 * rows * cols),
        name="decode",
    )(pos, outer, inner)


def sum_kernel(n, factor, blk_ref, *refs):
    total = refs[0][...].astype(F32)
    for ref in refs[1:n]:
        total = total + ref[...].astype(F32)
    if factor is not None:
        total = total * factor
    refs[n][...] = total.astype(refs[n].dtype)


def sum_of(pos, terms, rows, dtype, at=None, factor=None):
    width = terms[0].shape[1]
    n = len(terms)
    tile = rows // 2
    first = (lambda s: 0) if at is None else (lambda s: 2 * s[at])
    return pl.pallas_call(
        functools.partial(sum_kernel, n, factor),
        grid_spec=pltpu.PrefetchScalarGridSpec(
            num_scalar_prefetch=1,
            grid=(2,),
            in_specs=[pl.BlockSpec((tile, width), lambda i, s: (first(s) + i, 0))] * n,
            out_specs=pl.BlockSpec((tile, width), lambda i, s: (i, 0)),
        ),
        out_shape=jax.ShapeDtypeStruct((rows, width), dtype),
        compiler_params=params(60),
        cost_estimate=cost(n * rows * width, 2 * (n + 1) * rows * width),
        name="sum",
    )(pos, *terms)


def fold_kernel(up_ref, a_ref, low_ref, b_ref, up_out, low_out):
    up_out[...] = (up_ref[...].astype(F32) + a_ref[...].astype(F32)).astype(BF16)
    low_out[...] = (low_ref[...].astype(F32) + b_ref[...].astype(F32)).astype(BF16)


def fold(up, a, low, b):
    rows, width = a.shape
    block = (rows, width // 2)
    upper, lower = pl.BlockSpec(block, lambda i: (0, i)), pl.BlockSpec(block, lambda i: (1, i))
    return pl.pallas_call(
        fold_kernel,
        grid=(2,),
        in_specs=[upper, upper, lower, upper],
        out_specs=[upper, lower],
        out_shape=[jax.ShapeDtypeStruct(up.shape, BF16)] * 2,
        input_output_aliases={0: 0, 2: 1},
        compiler_params=params(60),
        cost_estimate=cost(2 * rows * width, 12 * rows * width),
        name="fold",
    )(up, a, low, b)


def halves_kernel(a_ref, b_ref, up_ref, low_ref):
    total = (a_ref[...].astype(F32) + b_ref[...].astype(F32)).astype(BF16)
    step = pl.program_id(0)

    @pl.when(step == 0)
    def _():
        up_ref[...] = total

    @pl.when(step == 1)
    def _():
        low_ref[...] = total


def halves_of(a, b):
    rows, width = a.shape[0] // 2, a.shape[1]
    return pl.pallas_call(
        halves_kernel,
        grid=(2,),
        in_specs=[pl.BlockSpec((rows, width), lambda i: (i, 0))] * 2,
        out_specs=[whole((rows, width))] * 2,
        out_shape=[jax.ShapeDtypeStruct((rows, width), BF16)] * 2,
        compiler_params=params(60),
        cost_estimate=cost(2 * rows * width, 12 * rows * width),
        name="halves",
    )(a, b)


def pre_kernel(factor, n, has_sum, last, off_ref, *refs):
    refs = list(refs)
    pieces = [refs.pop(0) for _ in range(n)]
    x_refs = [[refs.pop(0) for _ in range(n)] for _ in range(2)]
    sums = [refs.pop(0) for _ in range(2)] if has_sum else [None, None]
    cots = [refs.pop(0) for _ in range(2)] if last else [None, None]
    for xs, sum_ref, cot_ref, out_ref in zip(x_refs, sums, cots, refs):
        pre = sum_ref[...] if has_sum else None
        for x_ref, piece in zip(xs, pieces):
            term = jnp.dot(x_ref[...], piece[...], preferred_element_type=F32)
            pre = term if pre is None else pre + term
        if last:
            pre = pre * factor
            sig = 0.5 + 0.5 * jnp.tanh(0.5 * pre)
            pre = (cot_ref[...].astype(F32) * sig * (1.0 + pre * (1.0 - sig))).astype(BF16)
        out_ref[...] = pre


def pre_of(factor, pos, x_pair, pieces, offs, sums=None, cots=None):
    toks, feats = x_pair[0].shape
    width = pieces[0].shape[1]
    depth = sum(p.shape[0] for p in pieces)
    tile = toks // 2
    n = len(pieces)
    rows = feats // (NZ * NY)
    row = pl.BlockSpec((tile, width), lambda i, s: (i, 0))
    x_specs = [
        pl.BlockSpec(
            (tile, p.shape[0]), lambda i, s, p=p, w=w: (i, place_of(w, s, p.shape[0], rows))
        )
        for p, w in zip(pieces, offs)
    ]
    in_specs = [whole(p.shape) for p in pieces] + x_specs + x_specs
    args = list(pieces) + [x_pair[0]] * n + [x_pair[1]] * n
    if sums is not None:
        in_specs += [row, row]
        args += list(sums)
    if cots is not None:
        in_specs += [pl.BlockSpec((tile, width), lambda i, s: (i, s[AT_CORE]))] * 2
        args += list(cots)
    last = cots is not None
    return pl.pallas_call(
        functools.partial(pre_kernel, factor, n, sums is not None, last),
        grid_spec=pltpu.PrefetchScalarGridSpec(
            num_scalar_prefetch=1,
            grid=(toks // tile,),
            in_specs=in_specs,
            out_specs=[row, row],
        ),
        out_shape=[jax.ShapeDtypeStruct((toks, width), BF16 if last else F32)] * 2,
        compiler_params=params(60),
        cost_estimate=cost(4 * toks * depth * width, 4 * toks * depth + 2 * depth * width + 8 * toks * width),
        name="slope" if last else "pre",
    )(pos, *args)


def wgrad_kernel(halves, blk_ref, xo_ref, xp_ref, so_ref, sp_ref, *out_refs):
    step = pl.program_id(0)
    dims = (((0,), (0,)), ((), ()))
    term = lax.dot_general(xo_ref[...], so_ref[...], dims, preferred_element_type=F32)
    term = term + lax.dot_general(xp_ref[...], sp_ref[...], dims, preferred_element_type=F32)
    term = term.astype(BF16)
    out_refs = list(out_refs)
    for k, halved in enumerate(halves):
        mine = [out_refs.pop(0) for _ in range(2 if halved else 1)]

        @pl.when(step == k)
        def _(mine=mine):
            at = 0
            for ref in mine:
                ref[...] = term[at:at + ref.shape[0]]
                at += ref.shape[0]


def wgrad_of(pos, at, halves, x_pair, slopes):
    toks, feats = x_pair[0].shape
    width = slopes[0].shape[1]
    n = len(halves)
    rows = feats // (NZ * NY)
    shapes = []
    for halved in halves:
        shapes += [(rows // 2, width)] * 2 if halved else [(rows, width)]
    outs = pl.pallas_call(
        functools.partial(wgrad_kernel, halves),
        grid_spec=pltpu.PrefetchScalarGridSpec(
            num_scalar_prefetch=1,
            grid=(n,),
            in_specs=[pl.BlockSpec((toks, rows), lambda i, s: (0, s[at + i]))] * 2
            + [whole((toks, width))] * 2,
            out_specs=[whole(s) for s in shapes],
        ),
        out_shape=[jax.ShapeDtypeStruct(s, BF16) for s in shapes],
        compiler_params=params(60),
        cost_estimate=cost(4 * toks * n * rows * width, 4 * toks * n * rows + 2 * n * rows * width),
        name="wgrad",
    )(pos, *x_pair, *slopes)
    outs = list(outs)
    return [[outs.pop(0) for _ in range(2)] if halved else outs.pop(0) for halved in halves]


def late_kernel(n, offs, rows, s_ref, xo_ref, xp_ref, so_ref, sp_ref, *refs):
    step = pl.program_id(0)
    m = len(offs)
    pieces, outs, part_ref = refs[:m], refs[m:m + n], refs[m + n]
    tile = part_ref.shape[0]

    @pl.when(step < n)
    def _():
        dims = (((0,), (0,)), ((), ()))
        term = lax.dot_general(xo_ref[...], so_ref[...], dims, preferred_element_type=F32)
        term = term + lax.dot_general(xp_ref[...], sp_ref[...], dims, preferred_element_type=F32)
        term = term.astype(BF16)
        for k, out_ref in enumerate(outs):
            @pl.when(step == k)
            def _(out_ref=out_ref):
                out_ref[...] = term

    @pl.when(step >= n)
    def _():
        dims = (((1,), (1,)), ((), ()))
        slope = sp_ref[pl.ds(pl.multiple_of((step - n) * tile, tile), tile), :]
        for where, piece in zip(offs, pieces):
            depth = piece.shape[0]
            cols = pl.ds(pl.multiple_of(place_of(where, s_ref, depth, rows) * depth, 256), depth)
            part_ref[:, cols] = lax.dot_general(
                slope, piece[...], dims, preferred_element_type=F32
            ).astype(BF16)


def late_of(pos, x_pair, slopes, offs, pieces):
    toks, feats = x_pair[0].shape
    width = slopes[0].shape[1]
    n = len(LATE)
    rows = feats // (NZ * NY)
    tile = toks // 2
    outs = pl.pallas_call(
        functools.partial(late_kernel, n, offs, rows),
        grid_spec=pltpu.PrefetchScalarGridSpec(
            num_scalar_prefetch=1,
            grid=(n + toks // tile,),
            in_specs=[pl.BlockSpec((toks, rows), lambda i, s: (0, s[AT_LATE + jnp.minimum(i, n - 1)]))] * 2
            + [whole((toks, width))] * 2
            + [whole(p.shape) for p in pieces],
            out_specs=[whole((rows, width))] * n
            + [pl.BlockSpec((tile, feats), lambda i, s: (jnp.maximum(i - n, 0), 0))],
        ),
        out_shape=[jax.ShapeDtypeStruct((rows, width), BF16)] * n
        + [jax.ShapeDtypeStruct((toks, feats), BF16)],
        compiler_params=params(60),
        cost_estimate=cost(
            2 * toks * (2 * n * rows + feats) * width, 4 * toks * feats + 4 * feats * width
        ),
        name="late",
    )(pos, *x_pair, *slopes, *pieces)
    return outs


def igrad_kernel(factor, offs, rows, has_term, pos_ref, s_ref, *refs):
    n = len(offs)
    out_ref = refs[-1]
    dims = (((1,), (1,)), ((), ()))
    for where, piece in zip(offs, refs):
        depth = piece.shape[0]
        cols = pl.ds(pl.multiple_of(place_of(where, pos_ref, depth, rows) * depth, 256), depth)
        total = lax.dot_general(s_ref[...], piece[...], dims, preferred_element_type=F32)
        if has_term:
            total = (total + refs[n][:, cols].astype(F32)) * factor
        out_ref[:, cols] = total.astype(BF16)


def igrad_of(factor, pos, offs, slope, pieces, term=None):
    toks, width = slope.shape
    feats = sum(p.shape[0] for p in pieces)
    tile = toks // 2
    extra = [] if term is None else [term]
    return pl.pallas_call(
        functools.partial(
            igrad_kernel, factor, offs, feats // (NZ * NY), term is not None
        ),
        grid_spec=pltpu.PrefetchScalarGridSpec(
            num_scalar_prefetch=1,
            grid=(toks // tile,),
            in_specs=[pl.BlockSpec((tile, width), lambda i, s: (i, 0))]
            + [whole(p.shape) for p in pieces]
            + [pl.BlockSpec((tile, feats), lambda i, s: (i, 0)) for _ in extra],
            out_specs=pl.BlockSpec((tile, feats), lambda i, s: (i, 0)),
        ),
        out_shape=jax.ShapeDtypeStruct((toks, feats), BF16),
        compiler_params=params(60),
        cost_estimate=cost(2 * toks * feats * width, 2 * toks * feats + 2 * feats * width),
        name="igrad",
    )(pos, slope, *pieces, *extra)


def by_core(core, mine, other, axis):
    return jnp.where(
        core == 0,
        jnp.concatenate([mine, other], axis=axis),
        jnp.concatenate([other, mine], axis=axis),
    )


def place_kernel(pos_ref, *refs):
    for k, part_ref in enumerate(refs[:-1]):
        @pl.when(pl.program_id(0) == k)
        def _(part_ref=part_ref):
            refs[-1][...] = part_ref[...]


def side_by_side(pos, parts):
    rows, width = parts[0].shape
    n = len(parts)
    return pl.pallas_call(
        place_kernel,
        grid_spec=pltpu.PrefetchScalarGridSpec(
            num_scalar_prefetch=1,
            grid=(n,),
            in_specs=[whole((rows, width))] * n,
            out_specs=pl.BlockSpec((rows, width), lambda i, p: (0, lax.rem(p[AT_X] + n - i, n))),
        ),
        out_shape=jax.ShapeDtypeStruct((rows, n * width), parts[0].dtype),
        compiler_params=params(60),
        cost_estimate=cost(0, 4 * n * rows * width),
        name="place",
    )(pos, *parts)


def hold(a, *deps):
    return lax.optimization_barrier((a,) + deps)[0]


def shards(tokens, cotangent, next_weight, inner_weight, outer_weight, momentum):
    toks, feats = tokens.shape
    factor = feats ** (-0.5)
    me = lax.axis_index("shard")
    z, y, core = me // (NY * NC), (me // NC) % NY, me % NC
    replica = lax.axis_index("replica")
    low = replica % NL

    blk = {(dz, dy): ((z + dz) % NZ) * NY + (y + dy) % NY for dz, dy in DIRS}
    rows = feats // (NZ * NY)
    half = rows // 2
    cols = next_weight.shape[2] // NC

    def offs(*dirs):
        return [(DIRS.index(d[:2]), d[2] if len(d) == 3 else 0) for d in dirs]

    pos = jnp.stack(
        [blk[d] for d in DIRS + EARLY + LATE + LAST] + [core, 1 - core, replica // NL]
    ).astype(jnp.int32)

    keep = lax.dynamic_slice_in_dim(next_weight[0], core * cols, cols, 1)
    give = lax.dynamic_slice_in_dim(next_weight[0], (1 - core) * cols, cols, 1)
    w00 = by_core(core, keep, to_core(give), 0)

    w30, w10, w01 = to_zp(w00), to_zm(w00), to_y(w00)
    x_pair = (tokens, to_core(hold(tokens, w00)))
    cots = (cotangent, to_core(hold(cotangent, w00)))
    dec = decode(pos, hold(outer_weight, w00), inner_weight)
    x1, x2, x3 = [to_x(hold(dec[dx], x_pair[1], cots[1]), dx) for dx in (1, 2, 3)]

    a20 = to_zp(hold(w30, w01, dec[0], x1)[:half])
    b20 = to_zm(hold(w10, w01, dec[0], x1)[half:])
    first, first_offs = [w00, w30, w10, w01], offs((0, 0), (3, 0), (1, 0), (0, 1))
    sums = pre_of(factor, pos, x_pair, first, first_offs)

    a21, b21 = to_y(hold(a20, sums[0])), to_y(hold(b20, sums[0]))
    w31, w11 = to_zp(hold(w01, sums[0], a20)), to_zm(hold(w01, sums[0], b20))
    share = momentum.shape[1]

    def share_of(a, which):
        return lax.dynamic_slice_in_dim(a, which * share, share, 1)

    second, second_offs = [a20, b20], offs((2, 0), (2, 0, 1))
    sums = pre_of(factor, pos, x_pair, second, second_offs, sums)
    x_terms = [hold(dec[0], sums[0]), x1, x2, x3]
    other = add(*[share_of(a, 1 - low) for a in x_terms]).astype(BF16)
    mine = add(*[share_of(a, low) for a in x_terms])
    outer_share = lax.dynamic_slice_in_dim(outer_weight, replica * share, share, 1)
    outer_share = hold(outer_share, sums[0])
    low_got = to_l(hold(other, mine, outer_share, a21, b21, w31, w11))
    third, third_offs = [w31, w11, a21, b21], offs((3, 1), (1, 1), (2, 1), (2, 1, 1))
    slopes = pre_of(factor, pos, x_pair, third, third_offs, sums, cots)
    average = (mine + hold(low_got, slopes[0]).astype(F32)) / (NX * NL)
    new_momentum = 0.9 * momentum + average
    new_outer = outer_share - 0.7 * (average + 0.9 * new_momentum)
    inner_share = new_outer.astype(BF16)
    inner_other = to_l(inner_share)

    early_slopes = (hold(slopes[0], inner_share), slopes[1])
    g31, g11, g21 = wgrad_of(pos, AT_EARLY, (False,) * 3, x_pair, early_slopes)
    inner_other = hold(inner_other, g21)
    inner_pair = by_core(low, inner_share, inner_other, 1)
    g31, g11, g21 = [hold(g, inner_other) for g in (g31, g11, g21)]
    e2 = to_x(inner_pair, 2)

    r31, r11, r21 = to_zm(g31), to_zp(g11), to_y(g21)
    late_slopes = (hold(slopes[0], inner_pair), slopes[1])
    pieces, piece_offs = first + second + third, first_offs + second_offs + third_offs
    g20, g01, g00, part = late_of(pos, x_pair, late_slopes, piece_offs, pieces)

    ha20, hb20 = halves_of(g20, hold(r21, r31, r11, e2))
    ra20, rb20 = to_zm(ha20), to_zp(hb20)
    part_got = to_core(hold(part, ha20))
    s01 = sum_of(pos, [g01, hold(r31, ha20, hb20), r11], rows, BF16)
    t01 = to_y(s01)
    last_slopes = (hold(slopes[0], ha20, hb20, s01), slopes[1])
    g30, g10 = wgrad_of(pos, AT_LAST, (False,) * 2, x_pair, last_slopes)

    s30, s10 = fold(g30, ra20, g10, rb20)
    t30, t10 = to_zm(s30), to_zp(s10)
    e1, e3 = [to_x(hold(inner_pair, s30), dx) for dx in (1, 3)]
    input_grad = igrad_of(
        factor, pos, piece_offs, hold(slopes[0], s30, s10), pieces, part_got
    )
    new_inner = side_by_side(pos, [hold(inner_pair, input_grad), e1, e2, e3])
    terms = [hold(g00, new_inner), t30, t10, t01]

    def rows_of(which, own):
        halves = [lax.dynamic_slice_in_dim(a, which * half, half, 0) for a in [own] + terms[1:]]
        return add(*halves) * factor

    give_rows = rows_of(1 - core, terms[0])
    keep_rows = rows_of(core, hold(terms[0], give_rows))
    weight_grad = by_core(core, keep_rows, to_core(give_rows.astype(BF16)).astype(F32), 1)[None]
    return (input_grad, weight_grad, new_outer, new_momentum, new_inner)


def solution(mesh):
    return jax.shard_map(
        shards,
        mesh=mesh,
        in_specs=(
            P(("replica", "shard"), None),
            P(("replica", "shard"), None),
            P("replica", "shard", None),
            P("replica", "shard", None),
            P("shard", None),
            P("shard", "replica"),
        ),
        out_specs=(
            P(("replica", "shard"), None),
            P("replica", "shard", None),
            P("shard", "replica"),
            P("shard", "replica"),
            P("shard", None),
        ),
        check_vma=False,
    )
```
